128 devices in a mesh: face: 16 (over z_lo, y, core), member: 8 (over z_hi, x).
Axes of the slice: x: 4, y: 4, z: 4 (z_hi: 2, z_lo: 2; z = z_hi * 2 + z_lo), core: 2. Of those that a mesh axis runs over, the one named last changes fastest.
Arguments:
- features: bfloat16 [16, 48, 16, 16, 256], P('member', 'face'), may hold values from -6 to 6
- observed: bfloat16 [48, 80, 256], P('face', None, 'member'), may hold values from -6 to 6
- conv_weights: bfloat16 [2304, 2, 256], P(('face', 'member')), may hold values from -0.125 to 0.125
- head_weight: bfloat16 [256, 80], P(('face', 'member')), may hold values from -0.375 to 0.375
- adjacency: int32 [48, 4, 3], replicated, may hold values from 0 to 47, as said below
- placement_map: int32 [48], replicated, may hold values from 0 to 47, each once
Outputs:
- conv_grads: float32 [2304, 2, 256], P(('face', 'member'))
- head_grad: float32 [256, 80], P(('face', 'member'))
The draws below stay inside these ranges and needn't reach their ends.
Inputs may be any that keep to these rules, and one draw needn't show every extreme that they name: `adjacency`: the table is the gluing of the 12 HEALPix base faces, each cut into 4 square tiles, under a labelling of the tiles drawn from the seed: entry [t, a] = (n, b, f) glues side a of tile t to side b of tile n, reversed when f is 1; the gluing is mutual (entry [n, b] is (t, a, f)) and never joins a side to itself. `placement_map`: each tile stands at exactly one slot.
All inputs are finite; a program needn't handle non-finite values.
Results may differ from the reference program's by a relative error of at most 0.0005.
Values may be sent and summed in bfloat16 or wider, within the bound.
No kernel may reach another device: no remote copies, remote signals or barrier semaphores. Data moves between devices by JAX's collectives and lax.ppermute only.
A program may use at most 128 MiB of HBM per device.

```python
import math
import jax
import jax.numpy as jnp
import numpy as np
from jax import lax

C = 256
VARS = 80
FACES = 12
TILES_FACE = 4
TILE = 16
MEMBERS = 16
TILE_TOTAL = 48


def face_gluing(face, side):
    cycle, pos = divmod(face, 4)
    if cycle == 0:
        table = [((pos - 1) % 4, 1, 1), ((pos + 1) % 4, 0, 1), (4 + (pos + 1) % 4, 0, 0), (4 + pos, 1, 0)]
    elif cycle == 1:
        table = [((pos - 1) % 4, 2, 0), (pos, 3, 0), (8 + pos, 0, 0), (8 + (pos - 1) % 4, 1, 0)]
    else:
        table = [(4 + pos, 2, 0), (4 + (pos + 1) % 4, 3, 0), (8 + (pos + 1) % 4, 3, 1), (8 + (pos - 1) % 4, 2, 1)]
    return table[side]


def tile_on_side(side, place, width):
    if side == 0:
        return (0, place)
    if side == 1:
        return (place, width - 1)
    if side == 2:
        return (width - 1, place)
    return (place, 0)


def canonical_table():
    width = math.isqrt(TILES_FACE)
    rows_out = []
    for face in range(FACES):
        for tile_row in range(width):
            for tile_col in range(width):
                base = face * width * width
                entry = []
                for side in range(4):
                    inside = [tile_row > 0, tile_col < width - 1, tile_row < width - 1, tile_col > 0][side]
                    if inside:
                        step_row = [-1, 0, 1, 0][side]
                        step_col = [0, 1, 0, -1][side]
                        entry.append([base + (tile_row + step_row) * width + tile_col + step_col, (side + 2) % 4, 0])
                    else:
                        place = tile_col if side in (0, 2) else tile_row
                        other_face, other_side, flip_bit = face_gluing(face, side)
                        if flip_bit == 1:
                            place = width - 1 - place
                        other_row, other_col = tile_on_side(other_side, place, width)
                        entry.append([other_face * width * width + other_row * width + other_col, other_side, flip_bit])
                rows_out.append(entry)
    return np.array(rows_out, dtype=np.int32)


def draw_adjacency(key, part):
    canonical_order = jnp.asarray(canonical_table())
    label_list = jax.random.permutation(jax.random.fold_in(key, 11), TILE_TOTAL).astype(jnp.int32)
    renumbered_labels = jnp.stack([label_list[canonical_order[:, :, 0]], canonical_order[:, :, 1], canonical_order[:, :, 2]], axis=-1).astype(jnp.int32)
    return jnp.zeros((TILE_TOTAL, 4, 3), jnp.int32).at[label_list].set(renumbered_labels)


def with_spikes(values, stream_key, source, target, shards_of, factor):
    owner, partner = [(jnp.arange(values.shape[axis_at]) // (values.shape[axis_at] // shards_of)).reshape([-1 if axis == axis_at else 1 for axis in range(values.ndim)]) for axis_at in (source, target)]
    chosen = jax.random.permutation(stream_key, shards_of)[partner]
    strong = (owner == chosen) | (owner == (partner + shards_of // 2) % shards_of)
    return jnp.where(strong, factor * values, values)


def levels(own_key, shape, pieces, least, largest):
    factor_of = 1.0
    for dim, parts in pieces:
        heights = jax.random.uniform(jax.random.fold_in(jax.random.fold_in(own_key, 6), dim), (parts,), jnp.float32, least / len(pieces), largest / len(pieces))
        factor_of = factor_of * jnp.repeat(jnp.exp(heights), shape[dim] // parts).reshape((-1,) + (1,) * (len(shape) - 1 - dim))
    return factor_of


def bell_draw(rng, extent, scale, reach, pieces=(), held_as=jnp.bfloat16):
    values = scale * jax.random.normal(rng, extent, jnp.float32)
    if pieces:
        values = values * levels(rng, extent, pieces, -0.22, 0.18)
    return jnp.clip(values, -reach, reach).astype(held_as)


def heavy_noise(own_key, dims, deviation, most, shards, heavy, kind=jnp.bfloat16):
    values = deviation * jax.random.normal(own_key, dims, jnp.float32)
    if shards:
        values = values * levels(own_key, dims, shards, -0.22, 0.18)
    return jnp.clip(with_spikes(values, jax.random.fold_in(own_key, 3), *heavy), -most, most).astype(kind)


def setup_inputs(seed: int = 0) -> dict:
    splits = jax.random.split(jax.random.key(seed), 7)
    features = heavy_noise(splits[0], (MEMBERS, TILE_TOTAL, TILE, TILE, C), 1.0, 6.0, ((0, 8), (1, 16)), (1, 4, 16, 2.0))
    observed = bell_draw(splits[1], (TILE_TOTAL, VARS, TILE * TILE), 1.0, 6.0, ((0, 16), (2, 8)))
    conv_weights = bell_draw(splits[2], (9 * C, 2, C), (9 * C) ** -0.5, 0.125, ((0, 128),))
    head_weight = bell_draw(splits[3], (C, VARS), C ** -0.5, 0.375, ((0, 128),))
    adjacency = draw_adjacency(jax.random.fold_in(splits[6], 71), 0)
    placement_map = jax.random.permutation(splits[5], TILE_TOTAL).astype(jnp.int32)
    return {"features": features, "observed": observed, "conv_weights": conv_weights, "head_weight": head_weight, "adjacency": adjacency, "placement_map": placement_map}


smooth_sq = 0.0625

def split_edges(grid_field):
    return jnp.stack([grid_field[:, :, 0], grid_field[:, :, :, -1], grid_field[:, :, -1], grid_field[:, :, :, 0]], axis=2)

def border_of(padded):
    return jnp.stack([padded[:, :, 0, 1:-1], padded[:, :, 1:-1, -1], padded[:, :, -1, 1:-1], padded[:, :, 1:-1, 0]], axis=2)

def surround(grid_field, border):
    ensemble_members, tile_count, height, tile_w, channels = grid_field.shape
    corner = jnp.zeros((ensemble_members, tile_count, 1, 1, channels), grid_field.dtype)
    top_row = jnp.concatenate([corner, border[:, :, 0][:, :, None], corner], axis=3)
    low_row = jnp.concatenate([corner, border[:, :, 2][:, :, None], corner], axis=3)
    middle = jnp.concatenate([border[:, :, 3][:, :, :, None], grid_field, border[:, :, 1][:, :, :, None]], axis=3)
    return jnp.concatenate([top_row, middle, low_row], axis=2)

def convolve(padded, weight):
    channels = weight.shape[1]
    height = padded.shape[2] - 2
    tile_w = padded.shape[3] - 2
    summed = None
    for tap_index in range(9):
        row_off, col_off = divmod(tap_index, 3)
        window = padded[:, :, row_off:row_off + height, col_off:col_off + tile_w, :]
        product_part = jnp.dot(window.reshape(-1, channels), weight[tap_index * channels:(tap_index + 1) * channels], preferred_element_type=jnp.float32)
        summed = product_part if summed is None else summed + product_part
    return summed.reshape(padded.shape[:2] + (height, tile_w, channels))

def transpose_conv(slope_in, weight):
    channels = weight.shape[1]
    ensemble_members, tile_count, height, tile_w, _ = slope_in.shape
    result = jnp.zeros((ensemble_members, tile_count, height + 2, tile_w + 2, channels), jnp.float32)
    flat_slope = slope_in.reshape(-1, channels)
    for tap_index in range(9):
        row_off, col_off = divmod(tap_index, 3)
        product_part = lax.dot_general(flat_slope, weight[tap_index * channels:(tap_index + 1) * channels], (((1,), (1,)), ((), ())), preferred_element_type=jnp.float32)
        result = result.at[:, :, row_off:row_off + height, col_off:col_off + tile_w, :].add(product_part.reshape(slope_in.shape))
    return result

def weight_slope(padded, slope_in):
    channels = slope_in.shape[-1]
    height = slope_in.shape[2]
    tile_w = slope_in.shape[3]
    flat_slope = slope_in.reshape(-1, channels)
    pieces_out = []
    for tap_index in range(9):
        row_off, col_off = divmod(tap_index, 3)
        window = padded[:, :, row_off:row_off + height, col_off:col_off + tile_w, :]
        pieces_out.append(lax.dot_general(window.reshape(-1, channels), flat_slope, (((0,), (0,)), ((), ())), preferred_element_type=jnp.float32))
    return jnp.concatenate(pieces_out, axis=0)

def dsilu(argument):
    sigmoid_v = jax.nn.sigmoid(argument)
    return sigmoid_v * (1.0 + argument * (1.0 - sigmoid_v))

def reference(features, observed, conv_weights, head_weight, adjacency, placement_map):
    ensemble_members, tile_count, height, tile_w, channels = features.shape
    slot_ids = jnp.arange(tile_count, dtype=jnp.int32)
    slot_of = lax.optimization_barrier(jnp.sum(slot_ids[:, None] * (placement_map[:, None] == slot_ids[None, :]).astype(jnp.int32), axis=0))
    entries = adjacency[placement_map]
    source_slot = slot_of[entries[:, :, 0]]
    source_side = entries[:, :, 1]
    flip_flags = entries[:, :, 2]

    def partner_borders(edges):
        picked = edges[:, source_slot, source_side]
        return jnp.where(flip_flags[None, :, :, None, None] == 1, picked[:, :, :, ::-1, :], picked)
    pad_in = surround(features, partner_borders(split_edges(features)))
    pre_one = convolve(pad_in, conv_weights[:, 0, :])
    act_one = jax.nn.silu(pre_one).astype(jnp.bfloat16)
    pad_mid = surround(act_one, partner_borders(split_edges(act_one)))
    pre_two = convolve(pad_mid, conv_weights[:, 1, :])
    act_two = jax.nn.silu(pre_two).astype(jnp.bfloat16)
    flat_two = act_two.reshape(ensemble_members, tile_count, height * tile_w, channels).astype(jnp.float32)
    outputs = jnp.einsum('mtpc,cv->mtvp', flat_two, head_weight.astype(jnp.float32)).astype(jnp.bfloat16)
    out_vals = outputs.astype(jnp.float32)
    obs_vals = observed.astype(jnp.float32)
    paired = jnp.zeros(out_vals.shape, jnp.float32)
    for column_j in range(ensemble_members):
        spread = out_vals - out_vals[column_j]
        paired = paired + spread * lax.rsqrt(spread * spread + smooth_sq)
    own_gap = out_vals - obs_vals[None]
    slope_out = ((own_gap * lax.rsqrt(own_gap * own_gap + smooth_sq) / ensemble_members - paired / (ensemble_members * ensemble_members)) / TILE).astype(jnp.bfloat16)
    slope_f = slope_out.astype(jnp.float32)
    head_grad = jnp.einsum('mtpc,mtvp->cv', flat_two, slope_f)
    back_two = jnp.einsum('mtvp,cv->mtpc', slope_f, head_weight.astype(jnp.float32)).reshape(ensemble_members, tile_count, height, tile_w, channels)
    slope_two = (back_two * dsilu(pre_two)).astype(jnp.bfloat16)
    grad_two = weight_slope(pad_mid, slope_two)
    pad_slope = transpose_conv(slope_two, conv_weights[:, 1, :]).astype(jnp.bfloat16)
    returned = partner_borders(border_of(pad_slope)).astype(jnp.float32)
    slope_mid = pad_slope[:, :, 1:-1, 1:-1].astype(jnp.float32)
    slope_mid = slope_mid.at[:, :, 0].add(returned[:, :, 0])
    slope_mid = slope_mid.at[:, :, :, -1].add(returned[:, :, 1])
    slope_mid = slope_mid.at[:, :, -1].add(returned[:, :, 2])
    slope_mid = slope_mid.at[:, :, :, 0].add(returned[:, :, 3])
    slope_one = (slope_mid * dsilu(pre_one)).astype(jnp.bfloat16)
    grad_one = weight_slope(pad_in, slope_one)
    return (jnp.stack([grad_one, grad_two], axis=1), head_grad)
```

```python
import jax
import jax.numpy as jnp
from jax import lax
from jax.experimental import pallas as pl
from jax.experimental.pallas import tpu as pltpu
from jax.sharding import Mesh
from jax.sharding import PartitionSpec as P

smooth_sq = 0.0625
BF = jnp.bfloat16
F32 = jnp.float32
FACE = ("zl", "y", "c")
MEM = ("zh", "x")


def swap(value, axes, size, k):
    return lax.ppermute(value, axes, [(i, i ^ k) for i in range(size)])


def by_place(pieces, index):
    pieces = list(pieces)
    bit = 1
    while bit < len(pieces):
        odd = (index & bit) != 0
        pieces = [jnp.where(odd, pieces[i ^ bit], pieces[i]) for i in range(len(pieces))]
        bit *= 2
    return pieces


def table_body(adj, placed, coords, tab, slot_of):
    zl, y, c = coords[0], coords[1], coords[2]

    def note(s, carry):
        slot_of[placed[s]] = s
        return carry

    lax.fori_loop(0, 48, note, 0)
    for t, (dz, dc) in enumerate(((0, 0), (0, 1), (1, 1), (1, 0))):
        first = 3 * (((zl ^ dz) * 4 + y) * 2 + (c ^ dc))

        def one(i, carry):
            tile = placed[first + (i >> 2)]
            base = (tile * 4 + (i & 3)) * 3
            source = slot_of[adj[base]]
            face = (source * 171) >> 9
            row = (source - 3 * face) * 4 + adj[base + 1]
            other_c = (face & 1) != c
            other_z = (face >> 3) != zl
            which = ((face >> 1) & 3) ^ y
            if t == 3:
                row = jnp.where(other_c, 12 + i, row)
                which = jnp.where(other_c, 4, which)
            if t == 0:
                row = jnp.where(other_c, i, row)
                which = jnp.where(other_c, 4, which)
                row = jnp.where(other_z, i, row)
                which = jnp.where(other_z, 5, which)
                tab[96 + i] = adj[base + 2]
            tab[t * 12 + i] = which
            tab[48 + t * 12 + i] = row
            return carry

        lax.fori_loop(0, 12, one, 0)


def make_table(adjacency, placement_map, coords):
    return pl.pallas_call(
        table_body,
        out_shape=jax.ShapeDtypeStruct((108,), jnp.int32),
        in_specs=[pl.BlockSpec(memory_space=pltpu.SMEM)] * 3,
        out_specs=pl.BlockSpec(memory_space=pltpu.SMEM),
        scratch_shapes=[pltpu.SMEM((48,), jnp.int32)],
        name="table",
    )(adjacency.reshape(-1), placement_map, coords)


def pick_body(first, count, flips, tab, *refs):
    out = refs[-1]
    refs = refs[:-1]
    for i in range(count):
        which = tab[first + i]
        row = tab[48 + first + i]
        for m in range(2):
            got = None
            for n, ref in enumerate(refs):
                part = ref[m, jnp.minimum(row, ref.shape[1] - 1)]
                got = part if got is None else jnp.where(which == n, part, got)
            if flips:
                r = lax.broadcasted_iota(jnp.int32, (16, 16), 0)
                q = lax.broadcasted_iota(jnp.int32, (16, 16), 1)
                goal = jnp.where(tab[96 + i] == 1, 15 - r, r)
                turn = (q == goal).astype(F32).astype(BF)
                got = jnp.dot(turn, got, preferred_element_type=F32).astype(BF)
            out[m, i] = got


def pick(tab, refs, first, count, flips=False):
    return pl.pallas_call(
        lambda *a: pick_body(first, count, flips, *a),
        out_shape=jax.ShapeDtypeStruct((2, count, 16, 256), BF),
        in_specs=[pl.BlockSpec(memory_space=pltpu.SMEM)]
        + [pl.BlockSpec(memory_space=pltpu.VMEM)] * len(refs),
        out_specs=pl.BlockSpec(memory_space=pltpu.VMEM),
        name=f"pick{first}",
    )(tab, *refs)


def rims_of(edges, tab):
    edges = edges.reshape(2, 12, 16, 256)
    near = [edges] + [swap(edges, "y", 4, k) for k in (1, 2, 3)]
    got_c = swap(pick(tab, near, 12, 24), "c", 2, 1)
    got_z = swap(pick(tab, near + [got_c], 36, 12), "zl", 2, 1)
    rims = pick(tab, near + [got_c, got_z], 0, 12, True)
    return rims.reshape(2, 3, 4, 16, 256)


def split_edges(field):
    return jnp.stack([field[:, :, 0], field[:, :, :, -1], field[:, :, -1], field[:, :, :, 0]], axis=2)


def surround(field, border):
    corner = jnp.zeros((2, 3, 1, 1, 256), field.dtype)
    top = jnp.concatenate([corner, border[:, :, 0][:, :, None], corner], axis=3)
    low = jnp.concatenate([corner, border[:, :, 2][:, :, None], corner], axis=3)
    middle = jnp.concatenate(
        [border[:, :, 3][:, :, :, None], field, border[:, :, 1][:, :, :, None]], axis=3
    )
    return jnp.concatenate([top, middle, low], axis=2)


def three_wide(padded, order):
    padded = padded.reshape(6, 18, 18, 256)
    return jnp.concatenate([padded[:, :, b : b + 16] for b in order], axis=-1)


def conv(wide, weight, order=(0, 1, 2)):
    total = None
    for n, a in enumerate(order):
        part = jnp.dot(
            wide[:, a : a + 16].reshape(1536, 768),
            weight[n * 768 : (n + 1) * 768],
            preferred_element_type=F32,
        )
        total = part if total is None else total + part
    return total


def weight_grad(wide, slope):
    parts = [
        lax.dot_general(
            wide[:, a : a + 16].reshape(1536, 768),
            slope,
            (((0,), (0,)), ((), ())),
            preferred_element_type=F32,
        )
        for a in range(3)
    ]
    return jnp.concatenate(parts, axis=0)


def dsilu(v):
    s = jax.nn.sigmoid(v)
    return s * (1.0 + v * (1.0 - s))


def gather_member(block, m):
    return jnp.stack(by_place([block] + [swap(block, MEM, 8, k) for k in range(1, 8)], m))


def gather_face(block, zl, y, c):
    pair = jnp.stack(by_place([block, swap(block, "zl", 2, 1)], zl))
    row = jnp.stack(by_place([pair] + [swap(pair, "y", 4, k) for k in (1, 2, 3)], y), axis=1)
    return jnp.stack(by_place([row, swap(row, "c", 2, 1)], c), axis=2)


def scatter_sum(grad, zl, y, c, m, rows):
    keep, give = by_place([grad[:, :, 0], grad[:, :, 1]], c)
    grad = keep + swap(give, "c", 2, 1)
    parts = by_place([grad[:, q] for q in range(4)], y)
    grad = parts[0] + sum(swap(parts[k], "y", 4, k) for k in (1, 2, 3))
    keep, give = by_place([grad[0], grad[1]], zl)
    grad = keep + swap(give, "zl", 2, 1)
    return grad


def scatter_member(blocks, m):
    parts = by_place([blocks[q] for q in range(8)], m)
    return parts[0] + sum(swap(parts[k], MEM, 8, k) for k in range(1, 8))


def g_of(v):
    return v * lax.rsqrt(v * v + smooth_sq)


def shards(features, observed, conv_weights, head_weight, adjacency, placement_map):
    zl, y, c = (lax.axis_index(n) for n in FACE)
    m = lax.axis_index(MEM)
    tab = make_table(adjacency, placement_map, jnp.stack([zl, y, c]).astype(jnp.int32))

    head_rows = jnp.pad(head_weight, ((0, 0), (0, 176)))
    mine = jnp.concatenate([conv_weights[:, 0], conv_weights[:, 1], head_rows], axis=0)
    mine = gather_member(mine, m)
    w_one = gather_face(mine[:, :18].reshape(144, 256), zl, y, c).reshape(2304, 256)
    second = jnp.concatenate([mine[:, 18:36].reshape(144, 256), mine[:, 36:].reshape(16, 256)], axis=0)
    second = gather_face(second, zl, y, c)
    w_two = second[:, :, :, :144].reshape(2304, 256)
    head = second[:, :, :, 144:, :80].reshape(256, 80)

    pad_in = surround(features, rims_of(split_edges(features), tab))
    wide_in = three_wide(pad_in, (0, 1, 2))
    pre_one = conv(wide_in, w_one)
    act_one = jax.nn.silu(pre_one).astype(BF).reshape(2, 3, 16, 16, 256)
    pad_mid = surround(act_one, rims_of(split_edges(act_one), tab))
    wide_mid = three_wide(pad_mid, (0, 1, 2))
    pre_two = conv(wide_mid, w_two)
    act_two = jax.nn.silu(pre_two).astype(BF)
    outputs = jnp.dot(act_two, head, preferred_element_type=F32).astype(BF)

    outputs = outputs.reshape(2, 3, 8, 32, 80)
    sent = by_place([outputs[:, :, q] for q in range(8)], m)
    vals = jnp.concatenate([sent[0]] + [swap(sent[k], MEM, 8, k) for k in range(1, 8)], axis=0)
    vals = vals.astype(F32)
    obs = jnp.swapaxes(observed, 1, 2).astype(F32)
    paired = jnp.sum(g_of(vals[:, None] - vals[None]), axis=1)
    slopes = ((g_of(vals - obs[None]) / 16 - paired / 256) / 16).astype(BF)
    back = [slopes[:2]] + [swap(slopes[2 * k : 2 * k + 2], MEM, 8, k) for k in range(1, 8)]
    slope_out = jnp.stack(by_place(back, m), axis=2).reshape(1536, 80)

    head_term = lax.dot_general(act_two, slope_out, (((0,), (0,)), ((), ())), preferred_element_type=F32)
    back_two = lax.dot_general(slope_out, head, (((1,), (1,)), ((), ())), preferred_element_type=F32)
    slope_two = (back_two * dsilu(pre_two)).astype(BF)

    taps = jnp.swapaxes(w_two.reshape(3, 3, 256, 256), 2, 3)
    lines = split_edges(slope_two.reshape(2, 3, 16, 16, 256))
    lines = jnp.pad(lines, ((0, 0), (0, 0), (0, 0), (1, 1), (0, 0)))
    lines = jnp.concatenate([lines[:, :, :, 2 - t : 18 - t] for t in range(3)], axis=-1)
    side_taps = (taps[0], taps[:, 2], taps[2], taps[:, 0])
    borders = jnp.stack(
        [
            jnp.dot(lines[:, :, s].reshape(96, 768), side_taps[s].reshape(768, 256), preferred_element_type=F32)
            .astype(BF)
            .reshape(2, 3, 16, 256)
            for s in range(4)
        ],
        axis=2,
    )
    returned = rims_of(borders, tab).astype(F32)
    grad_two = weight_grad(wide_mid, slope_two)
    second_sum = jnp.concatenate(
        [
            grad_two.reshape(2, 4, 2, 144, 256),
            jnp.pad(head_term, ((0, 0), (0, 176))).reshape(2, 4, 2, 16, 256),
        ],
        axis=3,
    )
    second_sum = scatter_sum(second_sum, zl, y, c, m, 20)

    padded = jnp.pad(slope_two.reshape(2, 3, 16, 16, 256), ((0, 0), (0, 0), (1, 1), (1, 1), (0, 0)))
    wide_slope = three_wide(padded, (2, 1, 0))
    inner = conv(wide_slope, taps.reshape(2304, 256), (2, 1, 0)).astype(BF).astype(F32)
    mid = inner.reshape(2, 3, 16, 16, 256)
    mid = mid + jnp.pad(returned[:, :, 0][:, :, None], ((0, 0), (0, 0), (0, 15), (0, 0), (0, 0)))
    mid = mid + jnp.pad(returned[:, :, 1][:, :, :, None], ((0, 0), (0, 0), (0, 0), (15, 0), (0, 0)))
    mid = mid + jnp.pad(returned[:, :, 2][:, :, None], ((0, 0), (0, 0), (15, 0), (0, 0), (0, 0)))
    mid = mid + jnp.pad(returned[:, :, 3][:, :, :, None], ((0, 0), (0, 0), (0, 0), (0, 15), (0, 0)))
    slope_one = (mid.reshape(1536, 256) * dsilu(pre_one)).astype(BF)
    grad_one = weight_grad(wide_in, slope_one)
    first_sum = scatter_sum(grad_one.reshape(2, 4, 2, 144, 256), zl, y, c, m, 18)
    blocks = jnp.concatenate(
        [first_sum.reshape(8, 18, 256), second_sum[:144].reshape(8, 18, 256), second_sum[144:].reshape(8, 2, 256)],
        axis=1,
    )
    done = scatter_member(blocks, m)
    return jnp.stack([done[:18], done[18:36]], axis=1), done[36:, :80]


def solution(mesh):
    fine = Mesh(mesh.devices.reshape(2, 4, 2, 2, 4), FACE + MEM)
    both = FACE + MEM
    in_specs = (P(MEM, FACE), P(FACE, None, MEM), P(both), P(both), P(), P())
    return jax.shard_map(
        shards, mesh=fine, in_specs=in_specs, out_specs=(P(both), P(both)), check_vma=False
    )
```

```python
import functools

import jax
import jax.numpy as jnp
from jax import lax
from jax.experimental import pallas as pl
from jax.experimental.pallas import tpu as pltpu
from jax.sharding import Mesh
from jax.sharding import PartitionSpec as P

smooth_sq = 0.0625
BF = jnp.bfloat16
F32 = jnp.float32
FACE = ("zl", "y", "c")
MEM = ("zh", "x")
CORE = ("zl", "y", "zh", "x")
SLOTS = 6


def swap(value, axes, size, k):
    return lax.ppermute(value, axes, [(i, i ^ k) for i in range(size)])


def by_place(pieces, index):
    pieces = list(pieces)
    bit = 1
    while bit < len(pieces):
        odd = (index & bit) != 0
        pieces = [jnp.where(odd, pieces[i ^ bit], pieces[i]) for i in range(len(pieces))]
        bit *= 2
    return pieces


def ones_in(v):
    v = v - ((v >> 1) & 0x5555)
    v = (v & 0x3333) + ((v >> 2) & 0x3333)
    v = (v + (v >> 4)) & 0x0F0F
    return (v + (v >> 8)) & 0x1F


def table_body(adj, placed, coords, tab, slot_of, marks, many):
    chip, c = coords[0] * 4 + coords[1], coords[2]
    me = chip * 2 + c

    def note(s, carry):
        slot_of[placed[s]] = s
        return carry

    lax.fori_loop(0, 48, note, 0)

    def clear(i, carry):
        marks[i] = 0
        many[i] = 0
        return carry

    lax.fori_loop(0, 128, clear, 0)

    def where_from(slot, side):
        base = (placed[slot] * 4 + side) * 3
        source = slot_of[adj[base]]
        face = (source * 171) >> 9
        return face, (source - 3 * face) * 4 + adj[base + 1], adj[base + 2]

    def mark(slot, most):
        face = (slot * 171) >> 9
        for side in range(4):
            goal, _, _ = where_from(slot, side)
            at = face * 8 + (goal >> 1)
            count = many[at] + 1
            many[at] = count
            marks[at] = marks[at] | (1 << ((slot - 3 * face) * 4 + side))
            most = jnp.where((goal >> 1) == (face >> 1), most, jnp.maximum(most, count))
        return most

    tab[72] = lax.fori_loop(0, 48, mark, 0)

    def one(i, carry):
        goal, _, flip = where_from(3 * me + (i >> 2), i & 3)
        at = me * 8 + (goal >> 1)
        rank = ones_in(marks[at] & ((1 << i) - 1))
        far = rank >= SLOTS
        place = (goal >> 1) * SLOTS + jnp.where(far, rank - SLOTS, rank)
        tab[48 + i] = jnp.where((goal >> 1) == chip, 200, jnp.where(far, 100 + place, place))
        tab[60 + i] = flip
        for t, core in enumerate((c, 1 - c)):
            face, row, _ = where_from(3 * (chip * 2 + core) + (i >> 2), i & 3)
            rank = ones_in(marks[face * 8 + chip] & ((1 << row) - 1))
            far = rank >= SLOTS
            local = (face >> 1) == chip
            which = jnp.where(local, 0, jnp.where(far, 2, 1))
            row = jnp.where(local, row, (face >> 1) * SLOTS + jnp.where(far, rank - SLOTS, rank))
            other = (face & 1) != c
            if t == 0:
                which = jnp.where(other, 3, which)
                row = jnp.where(other, i, row)
            else:
                which = jnp.where(other, 0, which)
                row = jnp.where(other, 0, row)
            tab[24 * t + i] = which
            tab[24 * t + 12 + i] = row
        return carry

    lax.fori_loop(0, 12, one, 0)


def make_table(adjacency, placement_map, coords):
    return pl.pallas_call(
        table_body,
        out_shape=jax.ShapeDtypeStruct((80,), jnp.int32),
        in_specs=[pl.BlockSpec(memory_space=pltpu.SMEM)] * 3,
        out_specs=pl.BlockSpec(memory_space=pltpu.SMEM),
        scratch_shapes=[pltpu.SMEM((n,), jnp.int32) for n in (48, 128, 128)],
        name="table",
    )(adjacency.reshape(-1), placement_map, coords)


def post_body(first, tab, edges, out):
    for i in range(12):
        place = tab[48 + i] - first

        @pl.when((place >= 0) & (place < 8 * SLOTS))
        def _():
            out[place] = edges[i]


def post(tab, edges, first):
    return pl.pallas_call(
        functools.partial(post_body, first),
        out_shape=jax.ShapeDtypeStruct((8 * SLOTS, 32, 256), BF),
        in_specs=[pl.BlockSpec(memory_space=pltpu.SMEM), pl.BlockSpec(memory_space=pltpu.VMEM)],
        out_specs=pl.BlockSpec(memory_space=pltpu.VMEM),
        name=f"post{first}",
    )(tab, edges)


def pick_body(first, flips, tab, *refs):
    out = refs[-1]
    refs = refs[:-1]
    for i in range(12):
        which = tab[first + i]
        row = tab[first + 12 + i]
        got = refs[0][jnp.minimum(row, 11)]
        for n, ref in enumerate(refs[1:], 1):
            got = jnp.where(which == n, ref[jnp.minimum(row, ref.shape[0] - 1)], got)
        if flips:
            r = lax.broadcasted_iota(jnp.int32, (32, 32), 0)
            q = lax.broadcasted_iota(jnp.int32, (32, 32), 1)
            goal = jnp.where(tab[60 + i] == 1, (r & 16) + 15 - (r & 15), r)
            turn = (q == goal).astype(F32).astype(BF)
            got = jnp.dot(turn, got, preferred_element_type=F32).astype(BF)
        out[i] = got


def pick(tab, refs, first, flips=False):
    return pl.pallas_call(
        functools.partial(pick_body, first, flips),
        out_shape=jax.ShapeDtypeStruct((12, 32, 256), BF),
        in_specs=[pl.BlockSpec(memory_space=pltpu.SMEM)]
        + [pl.BlockSpec(memory_space=pltpu.VMEM)] * len(refs),
        out_specs=pl.BlockSpec(memory_space=pltpu.VMEM),
        name=f"pick{first}",
    )(tab, *refs)


def trade(value, axes):
    return lax.all_to_all(value, axes, split_axis=0, concat_axis=0, tiled=True)


def rims_of(edges, tab):
    edges = edges.transpose(1, 2, 0, 3, 4).reshape(12, 32, 256)
    got = trade(post(tab, edges, 0), ("zl", "y"))
    rest = lax.cond(
        tab[72] > SLOTS,
        lambda e, g: trade(post(tab, e, 100), ("zl", "y")),
        lambda e, g: g,
        edges,
        got,
    )
    near = [edges, got, rest]
    from_core = swap(pick(tab, near, 24), "c", 2, 1)
    rims = pick(tab, near + [from_core], 0, True)
    return rims.reshape(3, 4, 2, 16, 256).transpose(2, 0, 1, 3, 4)


def split_edges(field):
    return jnp.stack([field[:, :, 0], field[:, :, :, -1], field[:, :, -1], field[:, :, :, 0]], axis=2)


def surround(field, border):
    corner = jnp.zeros((2, 3, 1, 1, 256), field.dtype)
    top = jnp.concatenate([corner, border[:, :, 0][:, :, None], corner], axis=3)
    low = jnp.concatenate([corner, border[:, :, 2][:, :, None], corner], axis=3)
    middle = jnp.concatenate(
        [border[:, :, 3][:, :, :, None], field, border[:, :, 1][:, :, :, None]], axis=3
    )
    return jnp.concatenate([top, middle, low], axis=2)


def three_wide(padded, order):
    padded = padded.reshape(6, 18, 18, 256)
    return jnp.concatenate([padded[:, :, b : b + 16] for b in order], axis=-1)


def conv(wide, weight, order=(0, 1, 2)):
    total = None
    for n, a in enumerate(order):
        part = jnp.dot(
            wide[:, a : a + 16].reshape(1536, 768),
            weight[n * 768 : (n + 1) * 768],
            preferred_element_type=F32,
        )
        total = part if total is None else total + part
    return total


def weight_grad(wide, slope):
    parts = [
        lax.dot_general(
            wide[:, a : a + 16].reshape(1536, 768),
            slope,
            (((0,), (0,)), ((), ())),
            preferred_element_type=F32,
        )
        for a in range(3)
    ]
    return jnp.concatenate(parts, axis=0)


def dsilu(v):
    s = jax.nn.sigmoid(v)
    return s * (1.0 + v * (1.0 - s))


def both_cores(mine, c):
    pair = by_place([mine, swap(mine, "c", 2, 1)], c)
    return jnp.stack(pair, axis=1)


def scatter_sum(grad, c, rows):
    keep, give = by_place([grad[:, 0], grad[:, 1]], c)
    grad = keep + swap(give, "c", 2, 1)
    return jnp.sum(trade(grad.reshape(64, rows, 256), CORE), axis=0)


def g_of(v):
    return v * lax.rsqrt(v * v + smooth_sq)


def shards(features, observed, conv_weights, head_weight, adjacency, placement_map):
    zl, y, c = (lax.axis_index(n) for n in FACE)
    tab = make_table(adjacency, placement_map, jnp.stack([zl, y, c]).astype(jnp.int32))

    head_rows = jnp.pad(head_weight, ((0, 0), (0, 176)))
    mine = jnp.concatenate([conv_weights[:, 0], conv_weights[:, 1], head_rows], axis=0)
    mine = trade(jnp.broadcast_to(mine[None], (64, 38, 256)), CORE)
    w_one = both_cores(mine[:, :18].reshape(8, 144, 256), c).reshape(2304, 256)
    second = jnp.concatenate([mine[:, 18:36].reshape(8, 144, 256), mine[:, 36:].reshape(8, 16, 256)], axis=1)
    second = both_cores(second, c)
    w_two = second[:, :, :144].reshape(2304, 256)
    head = second[:, :, 144:, :80].reshape(256, 80)

    pad_in = surround(features, rims_of(split_edges(features), tab))
    wide_in = three_wide(pad_in, (0, 1, 2))
    pre_one = conv(wide_in, w_one)
    act_one = jax.nn.silu(pre_one).astype(BF).reshape(2, 3, 16, 16, 256)
    pad_mid = surround(act_one, rims_of(split_edges(act_one), tab))
    wide_mid = three_wide(pad_mid, (0, 1, 2))
    pre_two = conv(wide_mid, w_two)
    act_two = jax.nn.silu(pre_two).astype(BF)
    outputs = jnp.dot(act_two, head, preferred_element_type=F32).astype(BF)

    outputs = outputs.reshape(2, 3, 8, 32, 80).transpose(2, 0, 1, 3, 4)
    vals = trade(outputs, MEM).reshape(16, 3, 32, 80).astype(F32)
    obs = jnp.swapaxes(observed, 1, 2).astype(F32)
    paired = jnp.sum(g_of(vals[:, None] - vals[None]), axis=1)
    slopes = ((g_of(vals - obs[None]) / 16 - paired / 256) / 16).astype(BF)
    slope_out = trade(slopes.reshape(8, 2, 3, 32, 80), MEM).transpose(1, 2, 0, 3, 4).reshape(1536, 80)

    head_term = lax.dot_general(act_two, slope_out, (((0,), (0,)), ((), ())), preferred_element_type=F32)
    back_two = lax.dot_general(slope_out, head, (((1,), (1,)), ((), ())), preferred_element_type=F32)
    slope_two = (back_two * dsilu(pre_two)).astype(BF)

    taps = jnp.swapaxes(w_two.reshape(3, 3, 256, 256), 2, 3)
    lines = split_edges(slope_two.reshape(2, 3, 16, 16, 256))
    lines = jnp.pad(lines, ((0, 0), (0, 0), (0, 0), (1, 1), (0, 0)))
    lines = jnp.concatenate([lines[:, :, :, 2 - t : 18 - t] for t in range(3)], axis=-1)
    side_taps = (taps[0], taps[:, 2], taps[2], taps[:, 0])
    borders = jnp.stack(
        [
            jnp.dot(lines[:, :, s].reshape(96, 768), side_taps[s].reshape(768, 256), preferred_element_type=F32)
            .astype(BF)
            .reshape(2, 3, 16, 256)
            for s in range(4)
        ],
        axis=2,
    )
    returned = rims_of(borders, tab).astype(F32)
    grad_two = weight_grad(wide_mid, slope_two)
    blocks = jnp.concatenate(
        [
            grad_two.reshape(8, 2, 8, 18, 256),
            jnp.pad(head_term, ((0, 0), (0, 176))).reshape(8, 2, 8, 2, 256),
        ],
        axis=3,
    )
    second_sum = scatter_sum(blocks.reshape(8, 2, 160, 256), c, 20)

    padded = jnp.pad(slope_two.reshape(2, 3, 16, 16, 256), ((0, 0), (0, 0), (1, 1), (1, 1), (0, 0)))
    wide_slope = three_wide(padded, (2, 1, 0))
    inner = conv(wide_slope, taps.reshape(2304, 256), (2, 1, 0)).astype(BF).astype(F32)
    mid = inner.reshape(2, 3, 16, 16, 256)
    mid = mid + jnp.pad(returned[:, :, 0][:, :, None], ((0, 0), (0, 0), (0, 15), (0, 0), (0, 0)))
    mid = mid + jnp.pad(returned[:, :, 1][:, :, :, None], ((0, 0), (0, 0), (0, 0), (15, 0), (0, 0)))
    mid = mid + jnp.pad(returned[:, :, 2][:, :, None], ((0, 0), (0, 0), (15, 0), (0, 0), (0, 0)))
    mid = mid + jnp.pad(returned[:, :, 3][:, :, :, None], ((0, 0), (0, 0), (0, 0), (0, 15), (0, 0)))
    slope_one = (mid.reshape(1536, 256) * dsilu(pre_one)).astype(BF)
    grad_one = weight_grad(wide_in, slope_one)
    first_sum = scatter_sum(grad_one.reshape(8, 2, 144, 256), c, 18)
    return jnp.stack([first_sum, second_sum[:18]], axis=1), second_sum[18:, :80]


def solution(mesh):
    fine = Mesh(mesh.devices.reshape(2, 4, 2, 2, 4), FACE + MEM)
    both = FACE + MEM
    in_specs = (P(MEM, FACE), P(FACE, None, MEM), P(both), P(both), P(), P())
    return jax.shard_map(
        shards, mesh=fine, in_specs=in_specs, out_specs=(P(both), P(both)), check_vma=False
    )
```

```python
import functools

import jax
import jax.numpy as jnp
import ml_dtypes
import numpy as np
from jax import lax
from jax.experimental import pallas as pl
from jax.experimental.pallas import tpu as pltpu
from jax.sharding import Mesh
from jax.sharding import PartitionSpec as P

smooth_sq = 0.0625
BF = jnp.bfloat16
F32 = jnp.float32
FACE = ("zl", "y", "c")
MEM = ("zh", "x")
CORE = ("zl", "y", "zh", "x")
SLOTS = 6


def swap(value, axes, size, k):
    return lax.ppermute(value, axes, [(i, i ^ k) for i in range(size)])


def ones_in(v):
    v = v - ((v >> 1) & 0x5555)
    v = (v & 0x3333) + ((v >> 2) & 0x3333)
    v = (v + (v >> 4)) & 0x0F0F
    return (v + (v >> 8)) & 0x1F


def table_body(adj, placed, coords, tab, slot_of, marks, many):
    chip, c = coords[0] * 4 + coords[1], coords[2]
    me = chip * 2 + c

    def note(s, carry):
        slot_of[placed[s]] = s
        return carry

    lax.fori_loop(0, 48, note, 0)

    def clear(i, carry):
        marks[i] = 0
        many[i] = 0
        return carry

    lax.fori_loop(0, 128, clear, 0)

    def where_from(slot, side):
        base = (placed[slot] * 4 + side) * 3
        source = slot_of[adj[base]]
        face = (source * 171) >> 9
        return face, (source - 3 * face) * 4 + adj[base + 1], adj[base + 2]

    def mark(slot, most):
        face = (slot * 171) >> 9
        for side in range(4):
            goal, _, _ = where_from(slot, side)
            at = face * 8 + (goal >> 1)
            count = many[at] + 1
            many[at] = count
            marks[at] = marks[at] | (1 << ((slot - 3 * face) * 4 + side))
            most = jnp.where((goal >> 1) == (face >> 1), most, jnp.maximum(most, count))
        return most

    tab[72] = lax.fori_loop(0, 48, mark, 0)

    def one(i, carry):
        goal, _, flip = where_from(3 * me + (i >> 2), i & 3)
        at = me * 8 + (goal >> 1)
        rank = ones_in(marks[at] & ((1 << i) - 1))
        far = rank >= SLOTS
        place = (goal >> 1) * SLOTS + jnp.where(far, rank - SLOTS, rank)
        tab[48 + i] = jnp.where((goal >> 1) == chip, 200, jnp.where(far, 100 + place, place))
        tab[60 + i] = flip
        for t, core in enumerate((c, 1 - c)):
            face, row, _ = where_from(3 * (chip * 2 + core) + (i >> 2), i & 3)
            rank = ones_in(marks[face * 8 + chip] & ((1 << row) - 1))
            far = rank >= SLOTS
            local = (face >> 1) == chip
            which = jnp.where(local, 0, jnp.where(far, 2, 1))
            row = jnp.where(local, row, (face >> 1) * SLOTS + jnp.where(far, rank - SLOTS, rank))
            other = (face & 1) != c
            if t == 0:
                which = jnp.where(other, 3, which)
                row = jnp.where(other, i, row)
            else:
                which = jnp.where(other, 0, which)
                row = jnp.where(other, 0, row)
            tab[24 * t + i] = which
            tab[24 * t + 12 + i] = row
        return carry

    lax.fori_loop(0, 12, one, 0)


def make_table(adjacency, placement_map, coords):
    return pl.pallas_call(
        table_body,
        out_shape=jax.ShapeDtypeStruct((80,), jnp.int32),
        in_specs=[pl.BlockSpec(memory_space=pltpu.SMEM)] * 3,
        out_specs=pl.BlockSpec(memory_space=pltpu.SMEM),
        scratch_shapes=[pltpu.SMEM((n,), jnp.int32) for n in (48, 128, 128)],
        name="table",
    )(adjacency.reshape(-1), placement_map, coords)


def post_edges(tab, edges, out):
    for i in range(12):
        place = tab[48 + i]

        @pl.when(place < 8 * SLOTS)
        def _():
            out[place] = edges[i]


def post_rest_body(tab, edges, out):
    for i in range(12):
        place = tab[48 + i] - 100

        @pl.when((place >= 0) & (place < 8 * SLOTS))
        def _():
            out[place] = edges[i]


def choose(tab, first, i, refs):
    which = tab[first + i]
    row = tab[first + 12 + i]
    got = refs[0][jnp.minimum(row, 11)]
    for n, ref in enumerate(refs[1:], 1):
        got = jnp.where(which == n, ref[jnp.minimum(row, ref.shape[0] - 1)], got)
    return got


def pick_body(tab, edges, got, rest, out):
    for i in range(12):
        out[i] = choose(tab, 24, i, (edges, got, rest))


def rims_into(tab, refs, rim):
    r = lax.broadcasted_iota(jnp.int32, (32, 32), 0)
    q = lax.broadcasted_iota(jnp.int32, (32, 32), 1)
    for i in range(12):
        goal = jnp.where(tab[60 + i] == 1, (r & 16) + 15 - (r & 15), r)
        turn = (q == goal).astype(F32).astype(BF)
        line = dot(turn, choose(tab, 0, i, refs)).astype(BF)
        for m in range(2):
            rim[(i // 4) * 2 + m, (i % 4) * 16 : (i % 4) * 16 + 16] = line[m * 16 : m * 16 + 16]


def dot(a, b, dims=((1,), (0,))):
    return lax.dot_general(a, b, (dims, ((), ())), preferred_element_type=F32)


def constants():
    shift = np.zeros((2, 288, 320), np.float32)
    for n, step in enumerate((-1, 1)):
        for i in range(-1, 17):
            for j in range(16):
                k, row = j + step, (i + 1) * 16 + j
                inside = 0 <= k < 16
                if i == -1 or i == 16:
                    if inside:
                        shift[n, row, 256 + (0 if i < 0 else 32) + k] = 1
                elif inside:
                    shift[n, row, i * 16 + k] = 1
                else:
                    shift[n, row, 256 + (48 if k < 0 else 16) + i] = 1
    cells = [
        [k for k in range(16)],
        [k * 16 + 15 for k in range(16)],
        [240 + k for k in range(16)],
        [k * 16 for k in range(16)],
    ]
    select = np.zeros((64, 256), np.float32)
    lines = np.zeros((192, 256), np.float32)
    for side in range(4):
        for k in range(16):
            select[side * 16 + k, cells[side][k]] = 1
            for t in range(3):
                if 0 <= k + 1 - t < 16:
                    lines[(side * 3 + t) * 16 + k, cells[side][k + 1 - t]] = 1
    return [
        a.astype(ml_dtypes.bfloat16)
        for a in (shift[:, :, :256], shift[:, :, 256:], select, lines, select.T)
    ]


def put_edges(t, edges, lines):
    m = t // 3
    s = t - 3 * m
    for side in range(4):
        edges[4 * s + side, pl.ds(pl.multiple_of(m * 16, 16), 16)] = lines[side * 16 : side * 16 + 16]


def sigmoid(v):
    return 1.0 / (1.0 + jnp.exp(-v))


def edges_body(tab, x, select, edges, sent):
    def tile(t, carry):
        put_edges(t, edges, dot(select[...], x[t]).astype(BF))
        return carry

    lax.fori_loop(0, 6, tile, 0)
    post_edges(tab, edges, sent)


def weights_body(mine, one, two, wide):
    for q in range(8):
        for r in range(8):
            block = mine[8 * q + r].astype(F32)
            wide[0, 18 * r : 18 * r + 18] = block[:18]
            wide[1, 18 * r : 18 * r + 18] = block[18:36]
            wide[1, 144 + 2 * r : 146 + 2 * r] = block[36:38]
        one[q] = wide[0, :144].astype(BF)
        two[q] = wide[1].astype(BF)


def conv_body(last, tab, core, x, edges, got, rest, cores, own, other, shift_x, shift_r, select, *refs):
    if last:
        wide, pre, act, weight, head, out, rim = refs
    else:
        wide, pre, act, edges_out, sent, weight, rim = refs
    c = core[0]
    for q in range(8):
        for part, k in ((own, c), (other, 1 - c)):
            at = pl.multiple_of((2 * q + k) * 144, 144)
            weight[pl.ds(at, 144)] = part[q, :144]
            if last:
                at = pl.multiple_of((2 * q + k) * 16, 16)
                head[pl.ds(at, 16)] = part[q, 144:160, :128]
    rims_into(tab, (edges, got, rest, cores), rim)

    def tile(t, carry):
        m = t // 3
        s = t - 3 * m
        r = rim[s * 2 + m]
        v = x[t]
        wide[t, :16, 256:512] = r[:16]
        wide[t, 16:272, 256:512] = v
        wide[t, 272:, 256:512] = r[32:48]
        for n in range(2):
            moved = dot(shift_x[n], v) + dot(shift_r[n], r)
            wide[t, :, 512 * n : 512 * n + 256] = moved.astype(BF)
        total = dot(wide[t, :256], weight[:768])
        total += dot(wide[t, 16:272], weight[768:1536])
        total += dot(wide[t, 32:], weight[1536:])
        pre[t] = total
        a = (total * sigmoid(total)).astype(BF)
        act[t] = a
        if last:
            o = dot(a, head[...]).astype(BF)
            for q in range(8):
                out[q, t] = o[32 * q : 32 * q + 32]
        else:
            put_edges(t, edges_out, dot(select[...], a).astype(BF))
        return carry

    lax.fori_loop(0, 6, tile, 0)
    if not last:
        post_edges(tab, edges_out, sent)


def score_body(vals, obs, out):
    for s in range(3):
        for h in range(2):
            rows = slice(16 * h, 16 * h + 16)
            y = [vals[k // 2, (k % 2) * 3 + s, rows].astype(F32) for k in range(16)]
            o = obs[s, rows].astype(F32)
            paired = [jnp.zeros((16, 128), F32) for _ in range(16)]
            for a in range(16):
                for b in range(a + 1, 16):
                    g = g_of(y[a] - y[b])
                    paired[a] = paired[a] + g
                    paired[b] = paired[b] - g
            for k in range(16):
                value = (g_of(y[k] - o) / 16 - paired[k] / 256) / 16
                out[k // 2, (k % 2) * 3 + s, rows] = value.astype(BF)


def slope_body(tab, slopes, head, act, pre, weight, lines, slope, head_grad, edges, sent, rows):
    head_grad[...] = jnp.zeros_like(head_grad)

    def tile(t, carry):
        m = t // 3
        s = t - 3 * m
        out = jnp.concatenate([slopes[q, t] for q in range(8)], axis=0)
        v = pre[t]
        g = sigmoid(v)
        b = (dot(out, head[...], ((1,), (1,))) * (g * (1.0 + v * (1.0 - g)))).astype(BF)
        slope[t] = b
        head_grad[...] += dot(act[t], out, ((0,), (0,)))
        line = dot(lines[...], b).astype(BF)
        at = pl.multiple_of((s * 2 + m) * 16, 16)
        for k in range(12):
            rows[k, pl.ds(at, 16)] = line[16 * k : 16 * k + 16]
        return carry

    lax.fori_loop(0, 6, tile, 0)
    for side, taps in enumerate(((0, 1, 2), (2, 5, 8), (6, 7, 8), (0, 3, 6))):
        total = sum(
            dot(rows[3 * side + t], weight[tap * 256 : tap * 256 + 256], ((1,), (1,)))
            for t, tap in enumerate(taps)
        ).astype(BF)
        for s in range(3):
            edges[4 * s + side] = total[32 * s : 32 * s + 32]
    post_edges(tab, edges, sent)


def grad_into(wide, slope, sums):
    for a in range(3):
        rows = slice(768 * a, 768 * a + 768)
        for t in range(6):
            part = dot(wide[t, 16 * a : 16 * a + 256], slope[t], ((0,), (0,)))
            if t == 0:
                sums[rows] = part
            else:
                sums[rows] += part


def split_cores(c, sums, keep, give):
    for q in range(8):
        keep[q, :144] = sums[pl.ds(pl.multiple_of((2 * q + c) * 144, 144), 144)]
        give[q, :144] = sums[pl.ds(pl.multiple_of((2 * q + 1 - c) * 144, 144), 144)]


def back_body(core, wide, slope, head_grad, weight, shift_x, keep, give, inner, sums, moved):
    c = core[0]
    grad_into(wide, slope, sums)
    split_cores(c, sums, keep, give)
    for q in range(8):
        for ref, k in ((keep, c), (give, 1 - c)):
            ref[q, 144:160, :128] = head_grad[pl.ds(pl.multiple_of((2 * q + k) * 16, 16), 16)]
            ref[q, 144:160, 128:] = jnp.zeros((16, 128), F32)

    def tile(t, carry):
        v = slope[t]
        moved[1, :16] = jnp.zeros((16, 256), BF)
        moved[1, 16:272] = v
        moved[1, 272:] = jnp.zeros((16, 256), BF)
        moved[0] = dot(shift_x[0], v).astype(BF)
        moved[2] = dot(shift_x[1], v).astype(BF)
        total = None
        for tap in range(9):
            a, b = tap // 3, tap % 3
            part = dot(
                moved[2 - b, 16 * (2 - a) : 16 * (2 - a) + 256],
                weight[tap * 256 : tap * 256 + 256],
                ((1,), (1,)),
            )
            total = part if total is None else total + part
        inner[t] = total.astype(BF)
        return carry

    lax.fori_loop(0, 6, tile, 0)


def first_body(tab, core, edges, got, rest, cores, inner, pre, wide, spread, keep, give, rim, slope, sums):
    rims_into(tab, (edges, got, rest, cores), rim)

    def tile(t, carry):
        m = t // 3
        s = t - 3 * m
        mid = inner[t].astype(F32) + dot(spread[...], rim[s * 2 + m])
        v = pre[t]
        g = sigmoid(v)
        slope[t] = (mid * (g * (1.0 + v * (1.0 - g)))).astype(BF)
        return carry

    lax.fori_loop(0, 6, tile, 0)
    grad_into(wide, slope, sums)
    split_cores(core[0], sums, keep, give)


def pack_body(keep_one, got_one, keep_two, got_two, out):
    for q in range(8):
        one = keep_one[q] + got_one[q]
        two = keep_two[q] + got_two[q]
        for r in range(8):
            out[8 * q + r, :18] = one[18 * r : 18 * r + 18]
            out[8 * q + r, 18:36] = two[18 * r : 18 * r + 18]
            out[8 * q + r, 36:38] = two[144 + 2 * r : 146 + 2 * r]


def add_body(parts, out):
    total = parts[0]
    for k in range(1, 64):
        total = total + parts[k]
    out[...] = total


def call(body, outs, scratch, scalars, *args, name):
    vmem = pl.BlockSpec(memory_space=pltpu.VMEM)
    return pl.pallas_call(
        body,
        out_shape=[jax.ShapeDtypeStruct(shape, kind) for shape, kind in outs],
        in_specs=[pl.BlockSpec(memory_space=pltpu.SMEM)] * scalars + [vmem] * (len(args) - scalars),
        out_specs=[vmem] * len(outs),
        scratch_shapes=[pltpu.VMEM(shape, kind) for shape, kind in scratch],
        compiler_params=pltpu.CompilerParams(vmem_limit_bytes=32 << 20),
        name=name,
    )(*args)


def trade(value, axes):
    return lax.all_to_all(value, axes, split_axis=0, concat_axis=0, tiled=True)


EDGES = ((12, 32, 256), BF)
POST = ((8 * SLOTS, 32, 256), BF)
WIDE = ((6, 288, 768), BF)
PRE = ((6, 256, 256), F32)
ACT = ((6, 256, 256), BF)


def exchange(tab, edges, sent):
    got = trade(sent, ("zl", "y"))
    rest = lax.cond(
        tab[72] > SLOTS,
        lambda e, g: trade(call(post_rest_body, [POST], [], 1, tab, e, name="post_rest")[0], ("zl", "y")),
        lambda e, g: g,
        edges,
        got,
    )
    (wanted,) = call(pick_body, [EDGES], [], 1, tab, edges, got, rest, name="pick")
    return edges, got, rest, swap(wanted, "c", 2, 1)


def g_of(v):
    return v * lax.rsqrt(v * v + smooth_sq)


def shards(features, observed, conv_weights, head_weight, adjacency, placement_map):
    zl, y, c = (lax.axis_index(n) for n in FACE)
    core = jnp.reshape(c, (1,)).astype(jnp.int32)
    shift_x, shift_r, select, lines, spread = constants()

    head_rows = jnp.pad(head_weight, ((0, 0), (0, 176)))
    mine = jnp.concatenate([conv_weights[:, 0], conv_weights[:, 1], head_rows], axis=0)
    mine = trade(jnp.broadcast_to(mine[None], (64, 38, 256)), CORE)
    tab = make_table(adjacency, placement_map, jnp.stack([zl, y, c]).astype(jnp.int32))
    x = features.reshape(6, 256, 256)
    edges, sent = call(edges_body, [EDGES, POST], [], 1, tab, x, select, name="edges")
    near = exchange(tab, edges, sent)
    one, two = call(
        weights_body,
        [((8, 144, 256), BF), ((8, 160, 256), BF)],
        [((2, 160, 256), F32)],
        0,
        mine,
        name="weights",
    )
    one_too, two_too = swap(one, "c", 2, 1), swap(two, "c", 2, 1)

    wide_in, pre_one, act_one, edges, sent = call(
        functools.partial(conv_body, False),
        [WIDE, PRE, ACT, EDGES, POST],
        [((2304, 256), BF), ((6, 64, 256), BF)],
        2,
        *(tab, core, x, *near, one, one_too, shift_x, shift_r, select),
        name="conv_one",
    )
    near = exchange(tab, edges, sent)
    wide_mid, pre_two, act_two, weight, head, outputs = call(
        functools.partial(conv_body, True),
        [WIDE, PRE, ACT, ((2304, 256), BF), ((256, 128), BF), ((8, 6, 32, 128), BF)],
        [((6, 64, 256), BF)],
        2,
        *(tab, core, act_one, *near, two, two_too, shift_x, shift_r, select),
        name="conv_two",
    )
    vals = trade(outputs, MEM)
    obs = jnp.pad(jnp.swapaxes(observed, 1, 2), ((0, 0), (0, 0), (0, 48)))
    (slopes,) = call(score_body, [((8, 6, 32, 128), BF)], [], 0, vals, obs, name="score")
    slopes = trade(slopes, MEM)
    slope, head_grad, edges, sent = call(
        slope_body,
        [ACT, ((256, 128), F32), EDGES, POST],
        [((12, 96, 256), BF)],
        1,
        *(tab, slopes, head, act_two, pre_two, weight, lines),
        name="slope",
    )
    near = exchange(tab, edges, sent)
    keep_two, give_two, inner = call(
        back_body,
        [((8, 160, 256), F32), ((8, 160, 256), F32), ACT],
        [((2304, 256), F32), ((3, 288, 256), BF)],
        1,
        *(core, wide_mid, slope, head_grad, weight, shift_x),
        name="back",
    )
    got_two = swap(give_two, "c", 2, 1)
    keep_one, give_one = call(
        first_body,
        [((8, 144, 256), F32), ((8, 144, 256), F32)],
        [((6, 64, 256), BF), ((6, 256, 256), BF), ((2304, 256), F32)],
        2,
        *(tab, core, *near, inner, pre_one, wide_in, spread),
        name="first",
    )
    got_one = swap(give_one, "c", 2, 1)
    (packed,) = call(
        pack_body, [((64, 38, 256), F32)], [], 0, keep_one, got_one, keep_two, got_two, name="pack"
    )
    (done,) = call(add_body, [((38, 256), F32)], [], 0, trade(packed, CORE), name="add")
    return jnp.stack([done[:18], done[18:36]], axis=1), done[36:, :80]


def solution(mesh):
    fine = Mesh(mesh.devices.reshape(2, 4, 2, 2, 4), FACE + MEM)
    both = FACE + MEM
    in_specs = (P(MEM, FACE), P(FACE, None, MEM), P(both), P(both), P(), P())
    return jax.shard_map(
        shards, mesh=fine, in_specs=in_specs, out_specs=(P(both), P(both)), check_vma=False
    )
```

```python
import functools

import jax
import jax.numpy as jnp
from jax import lax
from jax.experimental import pallas as pl
from jax.experimental.pallas import tpu as pltpu
from jax.sharding import Mesh
from jax.sharding import PartitionSpec as P

smooth_sq = 0.0625
BF = jnp.bfloat16
F32 = jnp.float32
FACE = ("zl", "y", "c")
MEM = ("zh", "x")
CORE = ("zl", "y", "zh", "x")
SLOTS = 6
FIRST = 80
LATE = 176
OWN = 200


def swap(value, axes, size, k):
    return lax.ppermute(value, axes, [(i, i ^ k) for i in range(size)])


def ones_in(v):
    v = v - ((v >> 1) & 0x5555)
    v = (v & 0x3333) + ((v >> 2) & 0x3333)
    v = (v + (v >> 4)) & 0x0F0F
    return (v + (v >> 8)) & 0x1F


def table_body(adj, placed, coords, tab, slot_of, marks, many):
    chip, c = coords[0] * 4 + coords[1], coords[2]
    me = chip * 2 + c

    def note(s, carry):
        slot_of[placed[s]] = s
        return carry

    lax.fori_loop(0, 48, note, 0)

    def clear(i, carry):
        marks[i] = 0
        many[i] = 0
        return carry

    lax.fori_loop(0, 128, clear, 0)

    def where_from(slot, side):
        base = (placed[slot] * 4 + side) * 3
        source = slot_of[adj[base]]
        face = (source * 171) >> 9
        return face, (source - 3 * face) * 4 + adj[base + 1], adj[base + 2]

    def mark(slot, most):
        face = (slot * 171) >> 9
        for side in range(4):
            goal, _, _ = where_from(slot, side)
            at = face * 8 + (goal >> 1)
            count = many[at] + 1
            many[at] = count
            marks[at] = marks[at] | (1 << ((slot - 3 * face) * 4 + side))
            most = jnp.where((goal >> 1) == (face >> 1), most, jnp.maximum(most, count))
        return most

    tab[72] = lax.fori_loop(0, 48, mark, 0)

    def one(i, carry):
        goal, _, flip = where_from(3 * me + (i >> 2), i & 3)
        rank = ones_in(marks[me * 8 + (goal >> 1)] & ((1 << i) - 1))
        tab[48 + i] = jnp.where((goal >> 1) == chip, 255, (goal >> 1) * 16 + rank)
        tab[60 + i] = flip
        for t, core in enumerate((c, 1 - c)):
            face, row, _ = where_from(3 * (chip * 2 + core) + (i >> 2), i & 3)
            rank = ones_in(marks[face * 8 + chip] & ((1 << row) - 1))
            local = (face >> 1) == chip
            other = (face & 1) != c
            late = jnp.logical_not(local | other) & (rank >= SLOTS)
            at = (face >> 1) * SLOTS + rank
            which = jnp.where(local, 0, jnp.where(late, 3, 1))
            row = jnp.where(local, row, jnp.where(late, 12 * t + i, at))
            tab[LATE + 12 * t + i] = jnp.where(late, at - SLOTS, -1)
            tab[24 * t + i] = jnp.where(other, 2 if t == 0 else 0, which)
            tab[24 * t + 12 + i] = jnp.where(other, i if t == 0 else 0, row)
        for t, (dz, dc) in enumerate(((0, 0), (0, 1), (1, 1), (1, 0))):
            slot = 3 * (((coords[0] ^ dz) * 4 + coords[1]) * 2 + (c ^ dc)) + (i >> 2)
            face, row, _ = where_from(slot, i & 3)
            which = ((face >> 1) & 3) ^ coords[1]
            other = (face & 1) != c
            if t == 0 or t == 3:
                which = jnp.where(other, 4, which)
                row = jnp.where(other, i if t == 0 else 12 + i, row)
            if t == 0:
                tab[OWN + i] = jnp.where((face >> 3) != coords[0], 1, 0)
                tab[OWN + 12 + i] = i
            tab[FIRST + t * 12 + i] = which
            tab[FIRST + 48 + t * 12 + i] = row
        return carry

    lax.fori_loop(0, 12, one, 0)


def make_table(adjacency, placement_map, coords):
    return pl.pallas_call(
        table_body,
        out_shape=jax.ShapeDtypeStruct((OWN + 24,), jnp.int32),
        in_specs=[pl.BlockSpec(memory_space=pltpu.SMEM)] * 3,
        out_specs=pl.BlockSpec(memory_space=pltpu.SMEM),
        scratch_shapes=[pltpu.SMEM((n,), jnp.int32) for n in (48, 128, 128)],
        name="table",
    )(adjacency.reshape(-1), placement_map, coords)


def post_edges(first, tab, edges, out):
    for i in range(12):
        code = tab[48 + i]
        rank = (code & 15) - first

        @pl.when((code != 255) & (rank >= 0) & (rank < SLOTS))
        def _():
            out[(code >> 4) * SLOTS + rank] = edges[i]


def late_body(tab, rest, out):
    for i in range(24):
        at = tab[LATE + i]

        @pl.when(at >= 0)
        def _():
            out[i] = rest[at]


def choose(tab, first, step, i, refs):
    which = tab[first + i]
    row = tab[first + step + i]
    got = refs[0][jnp.minimum(row, 11)]
    for n, ref in enumerate(refs[1:], 1):
        got = jnp.where(which == n, ref[jnp.minimum(row, ref.shape[0] - 1)], got)
    return got


def pick_body(first, step, tab, *refs):
    for i in range(refs[-1].shape[0]):
        refs[-1][i] = choose(tab, first, step, i, refs[:-1])


def rims_into(tab, first, step, refs, rim):
    r = lax.broadcasted_iota(jnp.int32, (32, 32), 0)
    q = lax.broadcasted_iota(jnp.int32, (32, 32), 1)
    for i in range(12):
        goal = jnp.where(tab[60 + i] == 1, (r & 16) + 15 - (r & 15), r)
        turn = (q == goal).astype(F32).astype(BF)
        line = dot(turn, choose(tab, first, step, i, refs)).astype(BF)
        for m in range(2):
            rim[(i // 4) * 2 + m, (i % 4) * 16 : (i % 4) * 16 + 16] = line[m * 16 : m * 16 + 16]


def dot(a, b, dims=((1,), (0,))):
    return lax.dot_general(a, b, (dims, ((), ())), preferred_element_type=F32)


def grid_of(rows, columns):
    return (
        lax.broadcasted_iota(jnp.int32, (rows, columns), 0),
        lax.broadcasted_iota(jnp.int32, (rows, columns), 1),
    )


def one_hot(mask):
    return mask.astype(F32).astype(BF)


def cell_of(side, k):
    return jnp.where(side == 0, k, jnp.where(side == 1, 16 * k + 15, jnp.where(side == 2, 240 + k, 16 * k)))


def select_rows(row, column):
    return one_hot(cell_of(row >> 4, row & 15) == column)


def line_rows():
    row, column = grid_of(192, 256)
    part = row >> 4
    side = (part * 11) >> 5
    k = (row & 15) + 1 - (part - 3 * side)
    return one_hot((k >= 0) & (k < 16) & (cell_of(side, k) == column))


def shift_rows(columns):
    row, column = grid_of(576, columns)
    n = jnp.where(row >= 288, 1, 0)
    r = row - 288 * n
    i = (r >> 4) - 1
    k = (r & 15) + 2 * n - 1
    inside = (k >= 0) & (k < 16)
    middle = (i >= 0) & (i < 16)
    if columns == 256:
        return one_hot(inside & middle & (column == 16 * i + k))
    ends = jnp.where(i < 0, k, 32 + k)
    sides = jnp.where(k < 0, 48 + i, 16 + i)
    outer = jnp.logical_not(middle) & inside & (column == ends)
    return one_hot(outer | (middle & jnp.logical_not(inside) & (column == sides)))


def put_edges(t, edges, lines):
    m = t // 3
    s = t - 3 * m
    for side in range(4):
        edges[4 * s + side, pl.ds(pl.multiple_of(m * 16, 16), 16)] = lines[side * 16 : side * 16 + 16]


def sigmoid(v):
    return 1.0 / (1.0 + jnp.exp(-v))


def edges_body(x, edges):
    select = select_rows(*grid_of(64, 256))

    def tile(t, carry):
        put_edges(t, edges, dot(select, x[t]).astype(BF))
        return carry

    lax.fori_loop(0, 6, tile, 0, unroll=True)


def weights_body(mine, one, two, wide):
    for q in range(8):
        for r in range(8):
            block = mine[8 * q + r].astype(F32)
            wide[0, 18 * r : 18 * r + 18] = block[:18]
            wide[1, 18 * r : 18 * r + 18] = block[18:36]
            wide[1, 144 + 2 * r : 146 + 2 * r] = block[36:38]
        one[q] = wide[0, :144].astype(BF)
        two[q] = wide[1].astype(BF)


def conv_body(last, count, tab, core, x, *refs):
    near, refs = refs[:count], refs[count:]
    own, other, *refs = refs
    if last:
        wide, pre, act, weight, head, out, rim, shift_x, shift_r = refs
    else:
        wide, pre, act, edges_out, sent, weight, rim, shift_x, shift_r = refs
        select = select_rows(*grid_of(64, 256))
    shift_x[...] = shift_rows(256)
    shift_r[...] = shift_rows(64)
    c = core[0]
    for q in range(8):
        for part, k in ((own, c), (other, 1 - c)):
            at = pl.multiple_of((2 * q + k) * 144, 144)
            weight[pl.ds(at, 144)] = part[q, :144]
            if last:
                at = pl.multiple_of((2 * q + k) * 16, 16)
                head[pl.ds(at, 16)] = part[q, 144:160, :128]
    rims_into(tab, *((0, 12) if last else (OWN, 12)), near, rim)
    for t in range(6):
        m, s = divmod(t, 3)
        r = rim[s * 2 + m]
        v = x[t]
        wide[t, :16, 256:512] = r[:16]
        wide[t, 16:272, 256:512] = v
        wide[t, 272:, 256:512] = r[32:48]
        moved = (dot(shift_x[...], v) + dot(shift_r[...], r)).astype(BF)
        wide[t, :, :256] = moved[:288]
        wide[t, :, 512:] = moved[288:]
    total = dot(wide[:, :256].reshape(1536, 768), weight[:768])
    total += dot(wide[:, 16:272].reshape(1536, 768), weight[768:1536])
    total += dot(wide[:, 32:].reshape(1536, 768), weight[1536:])
    pre[...] = total.reshape(6, 256, 256)
    for t in range(6):
        v = pre[t]
        act[t] = (v * sigmoid(v)).astype(BF)
        if not last:
            put_edges(t, edges_out, dot(select, act[t]).astype(BF))
    if not last:
        post_edges(0, tab, edges_out, sent)
    if last:
        o = dot(act[...].reshape(1536, 256), head[...]).astype(BF)
        for t in range(6):
            for q in range(8):
                out[q, t] = o[256 * t + 32 * q : 256 * t + 32 * q + 32]


def score_body(vals, obs, out):
    for s in range(3):
        for h in range(2):
            rows = slice(16 * h, 16 * h + 16)
            y = [vals[k // 2, (k % 2) * 3 + s, rows].astype(F32) for k in range(16)]
            o = obs[s, rows].astype(F32)
            paired = [jnp.zeros((16, 128), F32) for _ in range(16)]
            for a in range(16):
                for b in range(a + 1, 16):
                    g = g_of(y[a] - y[b])
                    paired[a] = paired[a] + g
                    paired[b] = paired[b] - g
            for k in range(16):
                value = (g_of(y[k] - o) / 16 - paired[k] / 256) / 16
                out[k // 2, (k % 2) * 3 + s, rows] = value.astype(BF)


def slope_body(tab, slopes, head, act, pre, weight, slope, head_grad, edges, sent, rows, cells, lines):
    lines[...] = line_rows()
    for t in range(6):
        for q in range(8):
            cells[t, 32 * q : 32 * q + 32] = slopes[q, t]
    out = cells[...].reshape(1536, 128)
    head_grad[...] = dot(act[...].reshape(1536, 256), out, ((0,), (0,)))
    back = dot(out, head[...], ((1,), (1,)))
    for t in range(6):
        m, s = divmod(t, 3)
        v = pre[t]
        g = sigmoid(v)
        b = (back[256 * t : 256 * t + 256] * (g * (1.0 + v * (1.0 - g)))).astype(BF)
        slope[t] = b
        line = dot(lines[...], b).astype(BF)
        at = (s * 2 + m) * 16
        for k in range(12):
            rows[k, at : at + 16] = line[16 * k : 16 * k + 16]
    for side, taps in enumerate(((0, 1, 2), (2, 5, 8), (6, 7, 8), (0, 3, 6))):
        total = sum(
            dot(rows[3 * side + t], weight[tap * 256 : tap * 256 + 256], ((1,), (1,)))
            for t, tap in enumerate(taps)
        ).astype(BF)
        for s in range(3):
            edges[4 * s + side] = total[32 * s : 32 * s + 32]
    post_edges(0, tab, edges, sent)


def grad_into(wide, slope, sums):
    flat = slope[...].reshape(1536, 256)
    for a in range(3):
        sums[768 * a : 768 * a + 768] = dot(
            wide[:, 16 * a : 16 * a + 256].reshape(1536, 768), flat, ((0,), (0,))
        )


def split_cores(c, sums, keep, give):
    for q in range(8):
        keep[q] = sums[pl.ds(pl.multiple_of((2 * q + c) * 144, 144), 144)]
        give[q] = sums[pl.ds(pl.multiple_of((2 * q + 1 - c) * 144, 144), 144)]


def back_body(core, wide, slope, head_grad, weight, keep, give, inner, sums, moved, shift_x):
    c = core[0]
    grad_into(wide, slope, sums)
    for q in range(8):
        for ref, k in ((keep, c), (give, 1 - c)):
            block = sums[pl.ds(pl.multiple_of((2 * q + k) * 144, 144), 144)]
            rows = head_grad[pl.ds(pl.multiple_of((2 * q + k) * 16, 16), 16)]
            for r in range(8):
                ref[r, q, :18] = block[18 * r : 18 * r + 18]
                ref[r, q, 18:20, :128] = rows[2 * r : 2 * r + 2]
                ref[r, q, 18:20, 128:] = jnp.zeros((2, 128), F32)

    shift_x[...] = shift_rows(256)
    for t in range(6):
        v = slope[t]
        moved[1, t, :16] = jnp.zeros((16, 256), BF)
        moved[1, t, 16:272] = v
        moved[1, t, 272:] = jnp.zeros((16, 256), BF)
        both = dot(shift_x[...], v).astype(BF)
        moved[0, t] = both[:288]
        moved[2, t] = both[288:]
    total = None
    for tap in range(9):
        a, b = tap // 3, tap % 3
        part = dot(
            moved[2 - b, :, 16 * (2 - a) : 16 * (2 - a) + 256].reshape(1536, 256),
            weight[tap * 256 : tap * 256 + 256],
            ((1,), (1,)),
        )
        total = part if total is None else total + part
    inner[...] = total.astype(BF).reshape(6, 256, 256)


def first_body(tab, core, edges, got, cores, late, inner, pre, wide, keep, give, rim, slope, sums):
    column, row = grid_of(256, 64)
    spread = select_rows(row, column)
    rims_into(tab, 0, 12, (edges, got, cores, late), rim)

    def tile(t, carry):
        m = t // 3
        s = t - 3 * m
        mid = inner[t].astype(F32) + dot(spread, rim[s * 2 + m])
        v = pre[t]
        g = sigmoid(v)
        slope[t] = (mid * (g * (1.0 + v * (1.0 - g)))).astype(BF)
        return carry

    lax.fori_loop(0, 6, tile, 0, unroll=True)
    grad_into(wide, slope, sums)
    split_cores(core[0], sums, keep, give)


def pack_body(keep, got, keep_two, got_two, out):
    for q in range(8):
        one = keep[q] + got[q]
        for r in range(8):
            out[8 * q + r, :18] = one[18 * r : 18 * r + 18]
            out[8 * q + r, 18:38] = keep_two[r, q] + got_two[r, q]


def add_body(parts, out, last):
    total = parts[0]
    for k in range(1, 64):
        total = total + parts[k]
    out[...] = total[:18]
    last[...] = total[18:38]


def call(body, outs, scratch, scalars, *args, name, us=1):
    vmem = pl.BlockSpec(memory_space=pltpu.VMEM)
    return pl.pallas_call(
        body,
        out_shape=[jax.ShapeDtypeStruct(shape, kind) for shape, kind in outs],
        in_specs=[pl.BlockSpec(memory_space=pltpu.SMEM)] * scalars + [vmem] * (len(args) - scalars),
        out_specs=[vmem] * len(outs),
        scratch_shapes=[pltpu.VMEM(shape, kind) for shape, kind in scratch],
        compiler_params=pltpu.CompilerParams(vmem_limit_bytes=12 << 20),
        cost_estimate=pl.CostEstimate(flops=us * 1000000000, bytes_accessed=1000, transcendentals=0),
        name=name,
    )(*args)


def trade(value, axes):
    return lax.all_to_all(value, axes, split_axis=0, concat_axis=0, tiled=True)


EDGES = ((12, 32, 256), BF)
WIDE = ((6, 288, 768), BF)
PRE = ((6, 256, 256), F32)
ACT = ((6, 256, 256), BF)


SHIFTS = [((6, 64, 256), BF), ((576, 256), BF), ((576, 64), BF)]
POST = ((8 * SLOTS, 32, 256), BF)
SLOTS_LATE = ((24, 32, 256), BF)


def later(tab, edges):
    (sent,) = call(functools.partial(post_edges, SLOTS), [POST], [], 1, tab, edges, name="post_late")
    return call(late_body, [SLOTS_LATE], [], 1, tab, trade(sent, ("zl", "y")), name="late")[0]


def exchange(tab, edges, got):
    late = lax.cond(
        tab[72] > SLOTS, lambda e: later(tab, e), lambda e: jnp.zeros((24, 32, 256), BF), edges
    )
    refs = (edges, got, edges, late)
    (wanted,) = call(functools.partial(pick_body, 24, 12), [EDGES], [], 1, tab, *refs, name="pick")
    return edges, got, swap(wanted, "c", 2, 1), late


def exchange_all(tab, near):
    (wanted,) = call(
        functools.partial(pick_body, FIRST + 12, 48), [((24, 32, 256), BF)], [], 1, tab, *near, name="pick_c"
    )
    near.append(swap(wanted, "c", 2, 1))
    (wanted,) = call(functools.partial(pick_body, FIRST + 36, 48), [EDGES], [], 1, tab, *near, name="pick_z")
    (mine,) = call(functools.partial(pick_body, FIRST, 48), [EDGES], [], 1, tab, *near, name="pick_own")
    return [mine, swap(wanted, "zl", 2, 1)]


def g_of(v):
    return v * lax.rsqrt(v * v + smooth_sq)


def shards(features, observed, conv_weights, head_weight, adjacency, placement_map):
    zl, y, c, zh, x = (lax.axis_index(n) for n in FACE + MEM)
    core = jnp.stack([c, zh, x, y, zl]).astype(jnp.int32)
    tab = make_table(adjacency, placement_map, jnp.stack([zl, y, c]).astype(jnp.int32))
    fields = features.reshape(6, 256, 256)
    (edges,) = call(edges_body, [EDGES], [], 0, fields, name="edges", us=2)
    head_rows = jnp.pad(head_weight, ((0, 0), (0, 176)))
    mine = jnp.concatenate([conv_weights[:, 0], conv_weights[:, 1], head_rows], axis=0)
    near = [edges] + [swap(edges, "y", 4, k) for k in (1, 2, 3)]
    mine = jnp.broadcast_to(mine[None], (64, 38, 256))
    tab, mine, *near = lax.optimization_barrier((tab, mine, *near))
    mine = trade(mine, CORE)
    near = exchange_all(tab, near)
    obs = jnp.pad(jnp.swapaxes(observed, 1, 2), ((0, 0), (0, 0), (0, 48)))
    mine, obs, *near = lax.optimization_barrier((mine, obs, *near))
    one, two = call(
        weights_body,
        [((8, 144, 256), BF), ((8, 160, 256), BF)],
        [((2, 160, 256), F32)],
        0,
        mine,
        name="weights",
    )
    one_too, two_too = swap(one, "c", 2, 1), swap(two, "c", 2, 1)
    wide_in, pre_one, act_one, edges, sent = call(
        functools.partial(conv_body, False, 2),
        [WIDE, PRE, ACT, EDGES, POST],
        [((2304, 256), BF), *SHIFTS],
        2,
        *(tab, core, fields, *near, one, one_too),
        name="conv_one",
        us=7,
    )
    sent, two, two_too, obs = lax.optimization_barrier((sent, two, two_too, obs))
    near = exchange(tab, edges, trade(sent, ("zl", "y")))
    wide_mid, pre_two, act_two, weight, head, outputs = call(
        functools.partial(conv_body, True, 4),
        [WIDE, PRE, ACT, ((2304, 256), BF), ((256, 128), BF), ((8, 6, 32, 128), BF)],
        SHIFTS,
        2,
        *(tab, core, act_one, *near, two, two_too),
        name="conv_two",
        us=7,
    )
    vals = trade(outputs, MEM)
    (slopes,) = call(score_body, [((8, 6, 32, 128), BF)], [], 0, vals, obs, name="score")
    slopes = trade(slopes, MEM)
    slope, head_grad, edges, sent = call(
        slope_body,
        [ACT, ((256, 128), F32), EDGES, POST],
        [((12, 96, 256), BF), ((6, 256, 128), BF), ((192, 256), BF)],
        1,
        *(tab, slopes, head, act_two, pre_two, weight),
        name="slope",
        us=4,
    )
    got = trade(sent, ("zl", "y"))
    keep_two, give_two, inner = call(
        back_body,
        [((8, 8, 20, 256), F32), ((8, 8, 20, 256), F32), ACT],
        [((2304, 256), F32), ((3, 6, 288, 256), BF), ((576, 256), BF)],
        1,
        *(core, wide_mid, slope, head_grad, weight),
        name="back",
        us=6,
    )
    got, inner, keep_two, give_two = lax.optimization_barrier((got, inner, keep_two, give_two))
    near = exchange(tab, edges, got)
    got_two = swap(give_two, "c", 2, 1)
    keep_one, give_one = call(
        first_body,
        [((8, 144, 256), F32), ((8, 144, 256), F32)],
        [((6, 64, 256), BF), ((6, 256, 256), BF), ((2304, 256), F32)],
        2,
        *(tab, core, *near, inner, pre_one, wide_in),
        name="first",
        us=4,
    )
    got_one = swap(give_one, "c", 2, 1)
    (packed,) = call(
        pack_body, [((64, 38, 256), F32)], [], 0, keep_one, got_one, keep_two, got_two, name="pack"
    )
    first, second = call(add_body, [((18, 256), F32), ((20, 256), F32)], [], 0, trade(packed, CORE), name="add")
    return jnp.stack([first, second[:18]], axis=1), second[18:, :80]


def solution(mesh):
    fine = Mesh(mesh.devices.reshape(2, 4, 2, 2, 4), FACE + MEM)
    both = FACE + MEM
    in_specs = (P(MEM, FACE), P(FACE, None, MEM), P(both), P(both), P(), P())
    return jax.shard_map(
        shards, mesh=fine, in_specs=in_specs, out_specs=(P(both), P(both)), check_vma=False
    )
```

```python
import functools

import jax
import jax.numpy as jnp
from jax import lax
from jax.experimental import pallas as pl
from jax.experimental.pallas import tpu as pltpu
from jax.sharding import Mesh
from jax.sharding import PartitionSpec as P

smooth_sq = 0.0625
BF = jnp.bfloat16
F32 = jnp.float32
FACE = ("zl", "y", "c")
MEM = ("zh", "x")
CORE = ("zl", "y", "zh", "x")
SLOTS = 6
FIRST = 80
LATE = 176
OWN = 200


def swap(value, axes, size, k):
    return lax.ppermute(value, axes, [(i, i ^ k) for i in range(size)])


def ones_in(v):
    v = v - ((v >> 1) & 0x5555)
    v = (v & 0x3333) + ((v >> 2) & 0x3333)
    v = (v + (v >> 4)) & 0x0F0F
    return (v + (v >> 8)) & 0x1F


def table_body(adj, placed, coords, tab, slot_of, marks, many):
    chip, c = coords[0] * 4 + coords[1], coords[2]
    me = chip * 2 + c

    def note(s, carry):
        slot_of[placed[s]] = s
        return carry

    lax.fori_loop(0, 48, note, 0)

    def clear(i, carry):
        marks[i] = 0
        many[i] = 0
        return carry

    lax.fori_loop(0, 128, clear, 0)

    def where_from(slot, side):
        base = (placed[slot] * 4 + side) * 3
        source = slot_of[adj[base]]
        face = (source * 171) >> 9
        return face, (source - 3 * face) * 4 + adj[base + 1], adj[base + 2]

    def mark(slot, most):
        face = (slot * 171) >> 9
        for side in range(4):
            goal, _, _ = where_from(slot, side)
            at = face * 8 + (goal >> 1)
            count = many[at] + 1
            many[at] = count
            marks[at] = marks[at] | (1 << ((slot - 3 * face) * 4 + side))
            most = jnp.where((goal >> 1) == (face >> 1), most, jnp.maximum(most, count))
        return most

    tab[72] = lax.fori_loop(0, 48, mark, 0)

    def one(i, carry):
        goal, _, flip = where_from(3 * me + (i >> 2), i & 3)
        rank = ones_in(marks[me * 8 + (goal >> 1)] & ((1 << i) - 1))
        tab[48 + i] = jnp.where((goal >> 1) == chip, 255, (goal >> 1) * 16 + rank)
        tab[60 + i] = flip
        for t, core in enumerate((c, 1 - c)):
            face, row, _ = where_from(3 * (chip * 2 + core) + (i >> 2), i & 3)
            rank = ones_in(marks[face * 8 + chip] & ((1 << row) - 1))
            local = (face >> 1) == chip
            other = (face & 1) != c
            late = jnp.logical_not(local | other) & (rank >= SLOTS)
            at = (face >> 1) * SLOTS + rank
            which = jnp.where(local, 0, jnp.where(late, 3, 1))
            row = jnp.where(local, row, jnp.where(late, 12 * t + i, at))
            tab[LATE + 12 * t + i] = jnp.where(late, at - SLOTS, -1)
            tab[24 * t + i] = jnp.where(other, 2 if t == 0 else 0, which)
            tab[24 * t + 12 + i] = jnp.where(other, i if t == 0 else 0, row)
        for t, (dz, dc) in enumerate(((0, 0), (0, 1), (1, 1), (1, 0))):
            slot = 3 * (((coords[0] ^ dz) * 4 + coords[1]) * 2 + (c ^ dc)) + (i >> 2)
            face, row, _ = where_from(slot, i & 3)
            which = ((face >> 1) & 3) ^ coords[1]
            other = (face & 1) != c
            if t == 0 or t == 3:
                which = jnp.where(other, 4, which)
                row = jnp.where(other, i if t == 0 else 12 + i, row)
            if t == 0:
                tab[OWN + i] = jnp.where((face >> 3) != coords[0], 1, 0)
                tab[OWN + 12 + i] = i
            tab[FIRST + t * 12 + i] = which
            tab[FIRST + 48 + t * 12 + i] = row
        return carry

    lax.fori_loop(0, 12, one, 0)


def make_table(adjacency, placement_map, coords):
    return pl.pallas_call(
        table_body,
        out_shape=jax.ShapeDtypeStruct((OWN + 24,), jnp.int32),
        in_specs=[pl.BlockSpec(memory_space=pltpu.SMEM)] * 3,
        out_specs=pl.BlockSpec(memory_space=pltpu.SMEM),
        scratch_shapes=[pltpu.SMEM((n,), jnp.int32) for n in (48, 128, 128)],
        name="table",
    )(adjacency.reshape(-1), placement_map, coords)


def post_edges(first, tab, edges, out):
    for i in range(12):
        code = tab[48 + i]
        rank = (code & 15) - first

        @pl.when((code != 255) & (rank >= 0) & (rank < SLOTS))
        def _():
            out[(code >> 4) * SLOTS + rank] = edges[i]


def late_body(tab, rest, out):
    for i in range(24):
        at = tab[LATE + i]

        @pl.when(at >= 0)
        def _():
            out[i] = rest[at]


def choose(tab, first, step, i, refs):
    which = tab[first + i]
    row = tab[first + step + i]
    got = refs[0][jnp.minimum(row, 11)]
    for n, ref in enumerate(refs[1:], 1):
        got = jnp.where(which == n, ref[jnp.minimum(row, ref.shape[0] - 1)], got)
    return got


def pick_body(first, step, tab, *refs):
    for i in range(refs[-1].shape[0]):
        refs[-1][i] = choose(tab, first, step, i, refs[:-1])


def rims_into(tab, first, step, refs, rim):
    r = lax.broadcasted_iota(jnp.int32, (32, 32), 0)
    q = lax.broadcasted_iota(jnp.int32, (32, 32), 1)
    for i in range(12):
        goal = jnp.where(tab[60 + i] == 1, (r & 16) + 15 - (r & 15), r)
        turn = (q == goal).astype(F32).astype(BF)
        line = dot(turn, choose(tab, first, step, i, refs)).astype(BF)
        for m in range(2):
            rim[(i // 4) * 2 + m, (i % 4) * 16 : (i % 4) * 16 + 16] = line[m * 16 : m * 16 + 16]


def dot(a, b, dims=((1,), (0,))):
    return lax.dot_general(a, b, (dims, ((), ())), preferred_element_type=F32)


def grid_of(rows, columns):
    return (
        lax.broadcasted_iota(jnp.int32, (rows, columns), 0),
        lax.broadcasted_iota(jnp.int32, (rows, columns), 1),
    )


def one_hot(mask):
    return mask.astype(F32).astype(BF)


def cell_of(side, k):
    return jnp.where(side == 0, k, jnp.where(side == 1, 16 * k + 15, jnp.where(side == 2, 240 + k, 16 * k)))


def select_rows(row, column):
    return one_hot(cell_of(row >> 4, row & 15) == column)


def line_rows():
    row, column = grid_of(192, 256)
    part = row >> 4
    side = (part * 11) >> 5
    k = (row & 15) + 1 - (part - 3 * side)
    return one_hot((k >= 0) & (k < 16) & (cell_of(side, k) == column))


def shift_rows(columns):
    row, column = grid_of(576, columns)
    n = jnp.where(row >= 288, 1, 0)
    r = row - 288 * n
    i = (r >> 4) - 1
    k = (r & 15) + 2 * n - 1
    inside = (k >= 0) & (k < 16)
    middle = (i >= 0) & (i < 16)
    if columns == 256:
        return one_hot(inside & middle & (column == 16 * i + k))
    ends = jnp.where(i < 0, k, 32 + k)
    sides = jnp.where(k < 0, 48 + i, 16 + i)
    outer = jnp.logical_not(middle) & inside & (column == ends)
    return one_hot(outer | (middle & jnp.logical_not(inside) & (column == sides)))


def put_edges(t, edges, lines):
    m = t // 3
    s = t - 3 * m
    for side in range(4):
        edges[4 * s + side, pl.ds(pl.multiple_of(m * 16, 16), 16)] = lines[side * 16 : side * 16 + 16]


def sigmoid(v):
    return 1.0 / (1.0 + jnp.exp(-v))


def edges_body(x, edges):
    select = select_rows(*grid_of(64, 256))

    def tile(t, carry):
        put_edges(t, edges, dot(select, x[t]).astype(BF))
        return carry

    lax.fori_loop(0, 6, tile, 0, unroll=True)


def weights_body(mine, one, two, wide):
    for q in range(8):
        for r in range(8):
            block = mine[8 * q + r].astype(F32)
            wide[0, 18 * r : 18 * r + 18] = block[:18]
            wide[1, 18 * r : 18 * r + 18] = block[18:36]
            wide[1, 144 + 2 * r : 146 + 2 * r] = block[36:38]
        one[q] = wide[0, :144].astype(BF)
        two[q] = wide[1].astype(BF)


def conv_body(last, count, tab, core, x, *refs):
    near, refs = refs[:count], refs[count:]
    own, other, *refs = refs
    if last:
        wide, pre, weight, head, out, act, rim, shift_x, shift_r = refs
    else:
        wide, pre, act, edges_out, sent, weight, rim, shift_x, shift_r = refs
        select = select_rows(*grid_of(64, 256))
    shift_x[...] = shift_rows(256)
    shift_r[...] = shift_rows(64)
    c = core[0]
    for q in range(8):
        for part, k in ((own, c), (other, 1 - c)):
            at = pl.multiple_of((2 * q + k) * 144, 144)
            weight[pl.ds(at, 144)] = part[q, :144]
            if last:
                at = pl.multiple_of((2 * q + k) * 16, 16)
                head[pl.ds(at, 16)] = part[q, 144:160, :128]
    rims_into(tab, *((0, 12) if last else (OWN, 12)), near, rim)
    for t in range(6):
        m, s = divmod(t, 3)
        r = rim[s * 2 + m]
        v = x[t]
        wide[t, :16, 256:512] = r[:16]
        wide[t, 16:272, 256:512] = v
        wide[t, 272:, 256:512] = r[32:48]
        moved = (dot(shift_x[...], v) + dot(shift_r[...], r)).astype(BF)
        wide[t, :, :256] = moved[:288]
        wide[t, :, 512:] = moved[288:]
    total = dot(wide[:, :256].reshape(1536, 768), weight[:768])
    total += dot(wide[:, 16:272].reshape(1536, 768), weight[768:1536])
    total += dot(wide[:, 32:].reshape(1536, 768), weight[1536:])
    pre[...] = total.reshape(6, 256, 256)
    for t in range(6):
        v = pre[t]
        act[t] = (v * sigmoid(v)).astype(BF)
        if not last:
            put_edges(t, edges_out, dot(select, act[t]).astype(BF))
    if not last:
        post_edges(0, tab, edges_out, sent)
    if last:
        o = dot(act[...].reshape(1536, 256), head[...]).astype(BF)
        for t in range(6):
            for q in range(8):
                out[q, t] = o[256 * t + 32 * q : 256 * t + 32 * q + 32]


def score_body(vals, obs, out):
    for s in range(3):
        for h in range(2):
            rows = slice(16 * h, 16 * h + 16)
            y = [vals[k // 2, (k % 2) * 3 + s, rows].astype(F32) for k in range(16)]
            o = obs[s, rows].astype(F32)
            paired = [jnp.zeros((16, 128), F32) for _ in range(16)]
            for a in range(16):
                for b in range(a + 1, 16):
                    g = g_of(y[a] - y[b])
                    paired[a] = paired[a] + g
                    paired[b] = paired[b] - g
            for k in range(16):
                value = (g_of(y[k] - o) / 16 - paired[k] / 256) / 16
                out[k // 2, (k % 2) * 3 + s, rows] = value.astype(BF)


def slope_body(tab, slopes, head, pre, weight, slope, head_grad, edges, sent, rows, cells, lines, act):
    lines[...] = line_rows()
    for t in range(6):
        for q in range(8):
            cells[t, 32 * q : 32 * q + 32] = slopes[q, t]
    out = cells[...].reshape(1536, 128)
    back = dot(out, head[...], ((1,), (1,)))
    for t in range(6):
        m, s = divmod(t, 3)
        v = pre[t]
        g = sigmoid(v)
        act[t] = (v * g).astype(BF)
        b = (back[256 * t : 256 * t + 256] * (g * (1.0 + v * (1.0 - g)))).astype(BF)
        slope[t] = b
        line = dot(lines[...], b).astype(BF)
        at = (s * 2 + m) * 16
        for k in range(12):
            rows[k, at : at + 16] = line[16 * k : 16 * k + 16]
    head_grad[...] = dot(act[...].reshape(1536, 256), out, ((0,), (0,)))
    for side, taps in enumerate(((0, 1, 2), (2, 5, 8), (6, 7, 8), (0, 3, 6))):
        total = sum(
            dot(rows[3 * side + t], weight[tap * 256 : tap * 256 + 256], ((1,), (1,)))
            for t, tap in enumerate(taps)
        ).astype(BF)
        for s in range(3):
            edges[4 * s + side] = total[32 * s : 32 * s + 32]
    post_edges(0, tab, edges, sent)


def grad_into(wide, slope, sums):
    flat = slope[...].reshape(1536, 256)
    for a in range(3):
        sums[768 * a : 768 * a + 768] = dot(
            wide[:, 16 * a : 16 * a + 256].reshape(1536, 768), flat, ((0,), (0,))
        )


def split_cores(c, sums, keep, give):
    for q in range(8):
        keep[q] = sums[pl.ds(pl.multiple_of((2 * q + c) * 144, 144), 144)]
        give[q] = sums[pl.ds(pl.multiple_of((2 * q + 1 - c) * 144, 144), 144)]


def back_body(core, wide, slope, head_grad, weight, keep, give, inner, sums, moved, shift_x):
    c = core[0]
    grad_into(wide, slope, sums)
    for q in range(8):
        for ref, k in ((keep, c), (give, 1 - c)):
            block = sums[pl.ds(pl.multiple_of((2 * q + k) * 144, 144), 144)]
            rows = head_grad[pl.ds(pl.multiple_of((2 * q + k) * 16, 16), 16)]
            for r in range(8):
                ref[r, q, :18] = block[18 * r : 18 * r + 18]
                ref[r, q, 18:20, :128] = rows[2 * r : 2 * r + 2]
                ref[r, q, 18:20, 128:] = jnp.zeros((2, 128), F32)

    shift_x[...] = shift_rows(256)
    for t in range(6):
        v = slope[t]
        moved[1, t, :16] = jnp.zeros((16, 256), BF)
        moved[1, t, 16:272] = v
        moved[1, t, 272:] = jnp.zeros((16, 256), BF)
        both = dot(shift_x[...], v).astype(BF)
        moved[0, t] = both[:288]
        moved[2, t] = both[288:]
    total = None
    for tap in range(9):
        a, b = tap // 3, tap % 3
        part = dot(
            moved[2 - b, :, 16 * (2 - a) : 16 * (2 - a) + 256].reshape(1536, 256),
            weight[tap * 256 : tap * 256 + 256],
            ((1,), (1,)),
        )
        total = part if total is None else total + part
    inner[...] = total.astype(BF).reshape(6, 256, 256)


def first_body(tab, core, edges, got, cores, late, inner, pre, wide, keep, give, rim, slope, sums):
    column, row = grid_of(256, 64)
    spread = select_rows(row, column)
    rims_into(tab, 0, 12, (edges, got, cores, late), rim)

    def tile(t, carry):
        m = t // 3
        s = t - 3 * m
        mid = inner[t].astype(F32) + dot(spread, rim[s * 2 + m])
        v = pre[t]
        g = sigmoid(v)
        slope[t] = (mid * (g * (1.0 + v * (1.0 - g)))).astype(BF)
        return carry

    lax.fori_loop(0, 6, tile, 0, unroll=True)
    grad_into(wide, slope, sums)
    split_cores(core[0], sums, keep, give)


def pack_body(keep, got, keep_two, got_two, out):
    for q in range(8):
        one = keep[q] + got[q]
        for r in range(8):
            out[8 * q + r, :18] = one[18 * r : 18 * r + 18]
            out[8 * q + r, 18:38] = keep_two[r, q] + got_two[r, q]


def add_body(parts, out, last):
    total = parts[0]
    for k in range(1, 64):
        total = total + parts[k]
    out[:, 0, :] = total[:18]
    out[:, 1, :] = total[18:36]
    last[...] = total[36:38, :80]


def call(body, outs, scratch, scalars, *args, name, us=1):
    vmem = pl.BlockSpec(memory_space=pltpu.VMEM)
    return pl.pallas_call(
        body,
        out_shape=[jax.ShapeDtypeStruct(shape, kind) for shape, kind in outs],
        in_specs=[pl.BlockSpec(memory_space=pltpu.SMEM)] * scalars + [vmem] * (len(args) - scalars),
        out_specs=[vmem] * len(outs),
        scratch_shapes=[pltpu.VMEM(shape, kind) for shape, kind in scratch],
        compiler_params=pltpu.CompilerParams(vmem_limit_bytes=12 << 20),
        cost_estimate=pl.CostEstimate(flops=us * 1000000000, bytes_accessed=1000, transcendentals=0),
        name=name,
    )(*args)


def trade(value, axes):
    return lax.all_to_all(value, axes, split_axis=0, concat_axis=0, tiled=True)


EDGES = ((12, 32, 256), BF)
WIDE = ((6, 288, 768), BF)
PRE = ((6, 256, 256), F32)
ACT = ((6, 256, 256), BF)


SHIFTS = [((6, 64, 256), BF), ((576, 256), BF), ((576, 64), BF)]
POST = ((8 * SLOTS, 32, 256), BF)
SLOTS_LATE = ((24, 32, 256), BF)


def later(tab, edges):
    (sent,) = call(functools.partial(post_edges, SLOTS), [POST], [], 1, tab, edges, name="post_late")
    return call(late_body, [SLOTS_LATE], [], 1, tab, trade(sent, ("zl", "y")), name="late")[0]


def exchange(tab, over, edges, got):
    late = lax.cond(
        over, lambda e: later(tab, e), lambda e: jnp.zeros((24, 32, 256), BF), edges
    )
    refs = (edges, got, edges, late)
    (wanted,) = call(functools.partial(pick_body, 24, 12), [EDGES], [], 1, tab, *refs, name="pick")
    return edges, got, swap(wanted, "c", 2, 1), late


def exchange_all(tab, near):
    (wanted,) = call(
        functools.partial(pick_body, FIRST + 12, 48), [((24, 32, 256), BF)], [], 1, tab, *near, name="pick_c"
    )
    near.append(swap(wanted, "c", 2, 1))
    (wanted,) = call(functools.partial(pick_body, FIRST + 36, 48), [EDGES], [], 1, tab, *near, name="pick_z")
    (mine,) = call(functools.partial(pick_body, FIRST, 48), [EDGES], [], 1, tab, *near, name="pick_own")
    return [mine, swap(wanted, "zl", 2, 1)]


def g_of(v):
    return v * lax.rsqrt(v * v + smooth_sq)


def shards(features, observed, conv_weights, head_weight, adjacency, placement_map):
    zl, y, c, zh, x = (lax.axis_index(n) for n in FACE + MEM)
    core = jnp.stack([c, zh, x, y, zl]).astype(jnp.int32)
    head_rows = jnp.pad(head_weight, ((0, 0), (0, 176)))
    mine = jnp.concatenate([conv_weights[:, 0], conv_weights[:, 1], head_rows], axis=0)
    mine = jnp.broadcast_to(mine[None], (64, 38, 256))
    coords = jnp.stack([zl, y, c]).astype(jnp.int32)
    coords, mine = lax.optimization_barrier((coords, mine))
    tab = make_table(adjacency, placement_map, coords)
    fields = features.reshape(6, 256, 256)
    (edges,) = call(edges_body, [EDGES], [], 0, fields, name="edges", us=2)
    near = [edges] + [swap(edges, "y", 4, k) for k in (1, 2, 3)]
    tab, mine, *near = lax.optimization_barrier((tab, mine, *near))
    mine = trade(mine, CORE)
    near = exchange_all(tab, near)
    obs = jnp.pad(jnp.swapaxes(observed, 1, 2), ((0, 0), (0, 0), (0, 48)))
    over = tab[72] > SLOTS
    mine, obs, over, *near = lax.optimization_barrier((mine, obs, over, *near))
    one, two = call(
        weights_body,
        [((8, 144, 256), BF), ((8, 160, 256), BF)],
        [((2, 160, 256), F32)],
        0,
        mine,
        name="weights",
    )
    one_too, two_too = swap(one, "c", 2, 1), swap(two, "c", 2, 1)
    wide_in, pre_one, act_one, edges, sent = call(
        functools.partial(conv_body, False, 2),
        [WIDE, PRE, ACT, EDGES, POST],
        [((2304, 256), BF), *SHIFTS],
        2,
        *(tab, core, fields, *near, one, one_too),
        name="conv_one",
        us=7,
    )
    sent, two, two_too, obs = lax.optimization_barrier((sent, two, two_too, obs))
    near = exchange(tab, over, edges, trade(sent, ("zl", "y")))
    wide_mid, pre_two, weight, head, outputs = call(
        functools.partial(conv_body, True, 4),
        [WIDE, PRE, ((2304, 256), BF), ((256, 128), BF), ((8, 6, 32, 128), BF)],
        [ACT, *SHIFTS],
        2,
        *(tab, core, act_one, *near, two, two_too),
        name="conv_two",
        us=7,
    )
    vals = trade(outputs, MEM)
    (slopes,) = call(score_body, [((8, 6, 32, 128), BF)], [], 0, vals, obs, name="score")
    slopes = trade(slopes, MEM)
    slope, head_grad, edges, sent = call(
        slope_body,
        [ACT, ((256, 128), F32), EDGES, POST],
        [((12, 96, 256), BF), ((6, 256, 128), BF), ((192, 256), BF), ACT],
        1,
        *(tab, slopes, head, pre_two, weight),
        name="slope",
        us=4,
    )
    got = trade(sent, ("zl", "y"))
    keep_two, give_two, inner = call(
        back_body,
        [((8, 8, 20, 256), F32), ((8, 8, 20, 256), F32), ACT],
        [((2304, 256), F32), ((3, 6, 288, 256), BF), ((576, 256), BF)],
        1,
        *(core, wide_mid, slope, head_grad, weight),
        name="back",
        us=6,
    )
    got, inner = lax.optimization_barrier((got, inner))
    near = exchange(tab, over, edges, got)
    got_two = swap(give_two, "c", 2, 1)
    keep_one, give_one = call(
        first_body,
        [((8, 144, 256), F32), ((8, 144, 256), F32)],
        [((6, 64, 256), BF), ((6, 256, 256), BF), ((2304, 256), F32)],
        2,
        *(tab, core, *near, inner, pre_one, wide_in),
        name="first",
        us=4,
    )
    got_one = swap(give_one, "c", 2, 1)
    (packed,) = call(
        pack_body, [((64, 38, 256), F32)], [], 0, keep_one, got_one, keep_two, got_two, name="pack"
    )
    return call(add_body, [((18, 2, 256), F32), ((2, 80), F32)], [], 0, trade(packed, CORE), name="add")


def solution(mesh):
    fine = Mesh(mesh.devices.reshape(2, 4, 2, 2, 4), FACE + MEM)
    both = FACE + MEM
    in_specs = (P(MEM, FACE), P(FACE, None, MEM), P(both), P(both), P(), P())
    return jax.shard_map(
        shards, mesh=fine, in_specs=in_specs, out_specs=(P(both), P(both)), check_vma=False
    )
```

```python
import functools

import jax
import jax.numpy as jnp
from jax import lax
from jax.experimental import pallas as pl
from jax.experimental.pallas import tpu as pltpu
from jax.sharding import Mesh
from jax.sharding import PartitionSpec as P

smooth_sq = 0.0625
BF = jnp.bfloat16
F32 = jnp.float32
FACE = ("zl", "y", "c")
MEM = ("zh", "x")
CORE = ("zl", "y", "zh", "x")
SLOTS = 6
FIRST = 80
LATE = 176
OWN = 200


def swap(value, axes, size, k):
    return lax.ppermute(value, axes, [(i, i ^ k) for i in range(size)])


def ones_in(v):
    v = v - ((v >> 1) & 0x5555)
    v = (v & 0x3333) + ((v >> 2) & 0x3333)
    v = (v + (v >> 4)) & 0x0F0F
    return (v + (v >> 8)) & 0x1F


def table_body(adj, placed, coords, tab, slot_of, marks, many):
    chip, c = coords[0] * 4 + coords[1], coords[2]
    me = chip * 2 + c

    def note(s, carry):
        slot_of[placed[s]] = s
        return carry

    lax.fori_loop(0, 48, note, 0)

    def clear(i, carry):
        marks[i] = 0
        many[i] = 0
        return carry

    lax.fori_loop(0, 128, clear, 0)

    def where_from(slot, side):
        base = (placed[slot] * 4 + side) * 3
        source = slot_of[adj[base]]
        face = (source * 171) >> 9
        return face, (source - 3 * face) * 4 + adj[base + 1], adj[base + 2]

    def mark(slot, most):
        face = (slot * 171) >> 9
        for side in range(4):
            goal, _, _ = where_from(slot, side)
            at = face * 8 + (goal >> 1)
            count = many[at] + 1
            many[at] = count
            marks[at] = marks[at] | (1 << ((slot - 3 * face) * 4 + side))
            most = jnp.where((goal >> 1) == (face >> 1), most, jnp.maximum(most, count))
        return most

    tab[72] = lax.fori_loop(0, 48, mark, 0)

    def one(i, carry):
        goal, _, flip = where_from(3 * me + (i >> 2), i & 3)
        rank = ones_in(marks[me * 8 + (goal >> 1)] & ((1 << i) - 1))
        tab[48 + i] = jnp.where((goal >> 1) == chip, 255, (goal >> 1) * 16 + rank)
        tab[60 + i] = flip
        for t, core in enumerate((c, 1 - c)):
            face, row, _ = where_from(3 * (chip * 2 + core) + (i >> 2), i & 3)
            rank = ones_in(marks[face * 8 + chip] & ((1 << row) - 1))
            local = (face >> 1) == chip
            other = (face & 1) != c
            late = jnp.logical_not(local | other) & (rank >= SLOTS)
            at = (face >> 1) * SLOTS + rank
            which = jnp.where(local, 0, jnp.where(late, 3, 1))
            row = jnp.where(local, row, jnp.where(late, 12 * t + i, at))
            tab[LATE + 12 * t + i] = jnp.where(late, at - SLOTS, -1)
            tab[24 * t + i] = jnp.where(other, 2 if t == 0 else 0, which)
            tab[24 * t + 12 + i] = jnp.where(other, i if t == 0 else 0, row)
        for t, (dz, dc) in enumerate(((0, 0), (0, 1), (1, 1), (1, 0))):
            slot = 3 * (((coords[0] ^ dz) * 4 + coords[1]) * 2 + (c ^ dc)) + (i >> 2)
            face, row, _ = where_from(slot, i & 3)
            which = ((face >> 1) & 3) ^ coords[1]
            other = (face & 1) != c
            if t == 0 or t == 3:
                which = jnp.where(other, 4, which)
                row = jnp.where(other, i if t == 0 else 12 + i, row)
            if t == 0:
                tab[OWN + i] = jnp.where((face >> 3) != coords[0], 1, 0)
                tab[OWN + 12 + i] = i
            tab[FIRST + t * 12 + i] = which
            tab[FIRST + 48 + t * 12 + i] = row
        return carry

    lax.fori_loop(0, 12, one, 0)


def make_table(adjacency, placement_map, coords):
    return pl.pallas_call(
        table_body,
        out_shape=jax.ShapeDtypeStruct((OWN + 24,), jnp.int32),
        in_specs=[pl.BlockSpec(memory_space=pltpu.SMEM)] * 3,
        out_specs=pl.BlockSpec(memory_space=pltpu.SMEM),
        scratch_shapes=[pltpu.SMEM((n,), jnp.int32) for n in (48, 128, 128)],
        name="table",
    )(adjacency.reshape(-1), placement_map, coords)


def post_edges(first, tab, edges, out):
    for i in range(12):
        code = tab[48 + i]
        rank = (code & 15) - first

        @pl.when((code != 255) & (rank >= 0) & (rank < SLOTS))
        def _():
            out[(code >> 4) * SLOTS + rank] = edges[i]


def late_body(tab, rest, out):
    for i in range(24):
        at = tab[LATE + i]

        @pl.when(at >= 0)
        def _():
            out[i] = rest[at]


def choose(tab, first, step, i, refs):
    which = tab[first + i]
    row = tab[first + step + i]
    got = refs[0][jnp.minimum(row, 11)]
    for n, ref in enumerate(refs[1:], 1):
        got = jnp.where(which == n, ref[jnp.minimum(row, ref.shape[0] - 1)], got)
    return got


def pick_body(first, step, tab, *refs):
    for i in range(refs[-1].shape[0]):
        refs[-1][i] = choose(tab, first, step, i, refs[:-1])


def rims_into(tab, first, step, refs, rim):
    r = lax.broadcasted_iota(jnp.int32, (32, 32), 0)
    q = lax.broadcasted_iota(jnp.int32, (32, 32), 1)
    for i in range(12):
        goal = jnp.where(tab[60 + i] == 1, (r & 16) + 15 - (r & 15), r)
        turn = (q == goal).astype(F32).astype(BF)
        line = dot(turn, choose(tab, first, step, i, refs)).astype(BF)
        for m in range(2):
            rim[(i // 4) * 2 + m, (i % 4) * 16 : (i % 4) * 16 + 16] = line[m * 16 : m * 16 + 16]


def dot(a, b, dims=((1,), (0,))):
    return lax.dot_general(a, b, (dims, ((), ())), preferred_element_type=F32)


def grid_of(rows, columns):
    return (
        lax.broadcasted_iota(jnp.int32, (rows, columns), 0),
        lax.broadcasted_iota(jnp.int32, (rows, columns), 1),
    )


def one_hot(mask):
    return mask.astype(F32).astype(BF)


def cell_of(side, k):
    return jnp.where(side == 0, k, jnp.where(side == 1, 16 * k + 15, jnp.where(side == 2, 240 + k, 16 * k)))


def select_rows(row, column):
    return one_hot(cell_of(row >> 4, row & 15) == column)


def line_rows():
    row, column = grid_of(192, 256)
    part = row >> 4
    side = (part * 11) >> 5
    k = (row & 15) + 1 - (part - 3 * side)
    return one_hot((k >= 0) & (k < 16) & (cell_of(side, k) == column))


def shift_rows(columns):
    row, column = grid_of(576, columns)
    n = jnp.where(row >= 288, 1, 0)
    r = row - 288 * n
    i = (r >> 4) - 1
    k = (r & 15) + 2 * n - 1
    inside = (k >= 0) & (k < 16)
    middle = (i >= 0) & (i < 16)
    if columns == 256:
        return one_hot(inside & middle & (column == 16 * i + k))
    ends = jnp.where(i < 0, k, 32 + k)
    sides = jnp.where(k < 0, 48 + i, 16 + i)
    outer = jnp.logical_not(middle) & inside & (column == ends)
    return one_hot(outer | (middle & jnp.logical_not(inside) & (column == sides)))


def edge_rows(columns):
    row, column = grid_of(576, columns)
    tap = row >> 6
    down = (tap * 11) >> 5
    cell = cell_of((row >> 4) & 3, row & 15)
    i = (cell >> 4) + down - 1
    j = (cell & 15) + tap - 3 * down - 1
    in_i, in_j = (i >= 0) & (i < 16), (j >= 0) & (j < 16)
    if columns == 256:
        return one_hot(in_i & in_j & (column == 16 * i + j))
    ends = in_j & jnp.logical_not(in_i) & (column == jnp.where(i < 0, j, 32 + j))
    sides = in_i & jnp.logical_not(in_j) & (column == jnp.where(j < 0, 48 + i, 16 + i))
    return one_hot(ends | sides)


def put_edges(t, edges, lines):
    m = t // 3
    s = t - 3 * m
    for side in range(4):
        edges[4 * s + side, pl.ds(pl.multiple_of(m * 16, 16), 16)] = lines[side * 16 : side * 16 + 16]


def sigmoid(v):
    return 1.0 / (1.0 + jnp.exp(-v))


def edges_body(x, edges):
    select = select_rows(*grid_of(64, 256))

    def tile(t, carry):
        put_edges(t, edges, dot(select, x[t]).astype(BF))
        return carry

    lax.fori_loop(0, 6, tile, 0, unroll=True)


def weights_body(mine, one, two, wide):
    for q in range(8):
        for r in range(8):
            block = mine[8 * q + r].astype(F32)
            wide[0, 18 * r : 18 * r + 18] = block[:18]
            wide[1, 18 * r : 18 * r + 18] = block[18:36]
            wide[1, 144 + 2 * r : 146 + 2 * r] = block[36:38]
        one[q] = wide[0, :144].astype(BF)
        two[q] = wide[1].astype(BF)


def fill_weight(core, own, other, weight):
    c = core[0]
    for q in range(8):
        for part, k in ((own, c), (other, 1 - c)):
            weight[pl.ds(pl.multiple_of((2 * q + k) * 144, 144), 144)] = part[q, :144]


def sides_body(tab, core, x, a, b, own, other, edges, sent, seen, weight, rim, rows_x, rows_r):
    rows_x[...] = edge_rows(256)
    rows_r[...] = edge_rows(64)
    fill_weight(core, own, other, weight)
    rims_into(tab, OWN, 12, (a, b), rim)
    for t in range(6):
        m, s = divmod(t, 3)
        part = (dot(rows_x[...], x[t]) + dot(rows_r[...], rim[s * 2 + m])).astype(BF)
        for tap in range(9):
            seen[64 * t : 64 * t + 64, 256 * tap : 256 * tap + 256] = part[64 * tap : 64 * tap + 64]
    v = dot(seen[...], weight[...])
    line = (v * sigmoid(v)).astype(BF)
    for t in range(6):
        m, s = divmod(t, 3)
        for side in range(4):
            at = 64 * t + 16 * side
            edges[4 * s + side, 16 * m : 16 * m + 16] = line[at : at + 16]
    post_edges(0, tab, edges, sent)


def conv_body(last, keep, count, tab, core, x, *refs):
    near, refs = refs[:count], refs[count:]
    own, other, *refs = refs
    *refs, rim, shift_x, shift_r = refs
    if last and keep:
        wide, pre, weight, head = refs
    elif last:
        out, wide, pre, weight, head, act = refs
    elif keep:
        wide, pre, act, weight = refs
    else:
        edges_out, sent, wide, pre, act, weight = refs
        select = select_rows(*grid_of(64, 256))
    shift_x[...] = shift_rows(256)
    shift_r[...] = shift_rows(64)
    c = core[0]
    for q in range(8):
        for part, k in ((own, c), (other, 1 - c)):
            at = pl.multiple_of((2 * q + k) * 144, 144)
            weight[pl.ds(at, 144)] = part[q, :144]
            if last:
                at = pl.multiple_of((2 * q + k) * 16, 16)
                head[pl.ds(at, 16)] = part[q, 144:160, :128]
    rims_into(tab, *((0, 12) if last else (OWN, 12)), near, rim)
    for t in range(6):
        m, s = divmod(t, 3)
        r = rim[s * 2 + m]
        v = x[t]
        wide[t, :16, 256:512] = r[:16]
        wide[t, 16:272, 256:512] = v
        wide[t, 272:, 256:512] = r[32:48]
        moved = (dot(shift_x[...], v) + dot(shift_r[...], r)).astype(BF)
        wide[t, :, :256] = moved[:288]
        wide[t, :, 512:] = moved[288:]
    total = dot(wide[:, :256].reshape(1536, 768), weight[:768])
    total += dot(wide[:, 16:272].reshape(1536, 768), weight[768:1536])
    total += dot(wide[:, 32:].reshape(1536, 768), weight[1536:])
    pre[...] = total.reshape(6, 256, 256)
    if last and keep:
        return
    for t in range(6):
        v = pre[t]
        act[t] = (v * sigmoid(v)).astype(BF)
        if not last and not keep:
            put_edges(t, edges_out, dot(select, act[t]).astype(BF))
    if not last and not keep:
        post_edges(0, tab, edges_out, sent)
    if last:
        o = dot(act[...].reshape(1536, 256), head[...]).astype(BF)
        for t in range(6):
            for q in range(8):
                out[q, t] = o[256 * t + 32 * q : 256 * t + 32 * q + 32]


def score_body(vals, obs, out):
    for s in range(3):
        for h in range(2):
            rows = slice(16 * h, 16 * h + 16)
            y = [vals[k // 2, (k % 2) * 3 + s, rows].astype(F32) for k in range(16)]
            o = obs[s, rows].astype(F32)
            paired = [jnp.zeros((16, 128), F32) for _ in range(16)]
            for a in range(16):
                for b in range(a + 1, 16):
                    g = g_of(y[a] - y[b])
                    paired[a] = paired[a] + g
                    paired[b] = paired[b] - g
            for k in range(16):
                value = (g_of(y[k] - o) / 16 - paired[k] / 256) / 16
                out[k // 2, (k % 2) * 3 + s, rows] = value.astype(BF)


def slope_body(tab, slopes, head, pre, weight, slope, head_grad, edges, sent, rows, cells, lines, act):
    lines[...] = line_rows()
    for t in range(6):
        for q in range(8):
            cells[t, 32 * q : 32 * q + 32] = slopes[q, t]
    out = cells[...].reshape(1536, 128)
    back = dot(out, head[...], ((1,), (1,)))
    for t in range(6):
        m, s = divmod(t, 3)
        v = pre[t]
        g = sigmoid(v)
        act[t] = (v * g).astype(BF)
        b = (back[256 * t : 256 * t + 256] * (g * (1.0 + v * (1.0 - g)))).astype(BF)
        slope[t] = b
        line = dot(lines[...], b).astype(BF)
        at = (s * 2 + m) * 16
        for k in range(12):
            rows[k, at : at + 16] = line[16 * k : 16 * k + 16]
    head_grad[...] = dot(act[...].reshape(1536, 256), out, ((0,), (0,)))
    for side, taps in enumerate(((0, 1, 2), (2, 5, 8), (6, 7, 8), (0, 3, 6))):
        total = sum(
            dot(rows[3 * side + t], weight[tap * 256 : tap * 256 + 256], ((1,), (1,)))
            for t, tap in enumerate(taps)
        ).astype(BF)
        for s in range(3):
            edges[4 * s + side] = total[32 * s : 32 * s + 32]
    post_edges(0, tab, edges, sent)


def grad_into(wide, slope, sums):
    flat = slope[...].reshape(1536, 256)
    for a in range(3):
        sums[768 * a : 768 * a + 768] = dot(
            wide[:, 16 * a : 16 * a + 256].reshape(1536, 768), flat, ((0,), (0,))
        )


def split_cores(c, sums, keep, give):
    for q in range(8):
        keep[q] = sums[pl.ds(pl.multiple_of((2 * q + c) * 144, 144), 144)]
        give[q] = sums[pl.ds(pl.multiple_of((2 * q + 1 - c) * 144, 144), 144)]


def back_body(core, wide, slope, head_grad, weight, keep, give, inner, sums, moved, shift_x):
    c = core[0]
    grad_into(wide, slope, sums)
    for q in range(8):
        for ref, k in ((keep, c), (give, 1 - c)):
            block = sums[pl.ds(pl.multiple_of((2 * q + k) * 144, 144), 144)]
            rows = head_grad[pl.ds(pl.multiple_of((2 * q + k) * 16, 16), 16)]
            for r in range(8):
                ref[r, q, :18] = block[18 * r : 18 * r + 18]
                ref[r, q, 18:20, :128] = rows[2 * r : 2 * r + 2]
                ref[r, q, 18:20, 128:] = jnp.zeros((2, 128), F32)

    shift_x[...] = shift_rows(256)
    for t in range(6):
        v = slope[t]
        moved[1, t, :16] = jnp.zeros((16, 256), BF)
        moved[1, t, 16:272] = v
        moved[1, t, 272:] = jnp.zeros((16, 256), BF)
        both = dot(shift_x[...], v).astype(BF)
        moved[0, t] = both[:288]
        moved[2, t] = both[288:]
    total = None
    for tap in range(9):
        a, b = tap // 3, tap % 3
        part = dot(
            moved[2 - b, :, 16 * (2 - a) : 16 * (2 - a) + 256].reshape(1536, 256),
            weight[tap * 256 : tap * 256 + 256],
            ((1,), (1,)),
        )
        total = part if total is None else total + part
    inner[...] = total.astype(BF).reshape(6, 256, 256)


def first_body(tab, core, edges, got, cores, late, inner, pre, wide, keep, give, rim, slope, sums):
    column, row = grid_of(256, 64)
    spread = select_rows(row, column)
    rims_into(tab, 0, 12, (edges, got, cores, late), rim)

    def tile(t, carry):
        m = t // 3
        s = t - 3 * m
        mid = inner[t].astype(F32) + dot(spread, rim[s * 2 + m])
        v = pre[t]
        g = sigmoid(v)
        slope[t] = (mid * (g * (1.0 + v * (1.0 - g)))).astype(BF)
        return carry

    lax.fori_loop(0, 6, tile, 0, unroll=True)
    grad_into(wide, slope, sums)
    split_cores(core[0], sums, keep, give)


def pack_body(keep, got, keep_two, got_two, out):
    for q in range(8):
        one = keep[q] + got[q]
        for r in range(8):
            out[8 * q + r, :18] = one[18 * r : 18 * r + 18]
            out[8 * q + r, 18:38] = keep_two[r, q] + got_two[r, q]


def add_body(parts, out, last):
    total = parts[0]
    for k in range(1, 64):
        total = total + parts[k]
    out[:, 0, :] = total[:18]
    out[:, 1, :] = total[18:36]
    last[...] = total[36:38, :80]


def call(body, outs, scratch, scalars, *args, name, us=1):
    vmem = pl.BlockSpec(memory_space=pltpu.VMEM)
    return pl.pallas_call(
        body,
        out_shape=[jax.ShapeDtypeStruct(shape, kind) for shape, kind in outs],
        in_specs=[pl.BlockSpec(memory_space=pltpu.SMEM)] * scalars + [vmem] * (len(args) - scalars),
        out_specs=[vmem] * len(outs),
        scratch_shapes=[pltpu.VMEM(shape, kind) for shape, kind in scratch],
        compiler_params=pltpu.CompilerParams(vmem_limit_bytes=16 << 20),
        cost_estimate=pl.CostEstimate(flops=us * 1000000000, bytes_accessed=1000, transcendentals=0),
        name=name,
    )(*args)


def trade(value, axes):
    return lax.all_to_all(value, axes, split_axis=0, concat_axis=0, tiled=True)


EDGES = ((12, 32, 256), BF)
WIDE = ((6, 288, 768), BF)
PRE = ((6, 256, 256), F32)
ACT = ((6, 256, 256), BF)


WEIGHT = ((2304, 256), BF)
SHIFTS = [((6, 64, 256), BF), ((576, 256), BF), ((576, 64), BF)]
POST = ((8 * SLOTS, 32, 256), BF)
SLOTS_LATE = ((24, 32, 256), BF)


def later(tab, edges):
    (sent,) = call(functools.partial(post_edges, SLOTS), [POST], [], 1, tab, edges, name="post_late")
    return call(late_body, [SLOTS_LATE], [], 1, tab, trade(sent, ("zl", "y")), name="late")[0]


def exchange(tab, over, edges, got):
    late = lax.cond(
        over, lambda e: later(tab, e), lambda e: jnp.zeros((24, 32, 256), BF), edges
    )
    refs = (edges, got, edges, late)
    (wanted,) = call(functools.partial(pick_body, 24, 12), [EDGES], [], 1, tab, *refs, name="pick")
    return edges, got, swap(wanted, "c", 2, 1), late


def exchange_all(tab, near):
    (wanted,) = call(
        functools.partial(pick_body, FIRST + 12, 48), [((24, 32, 256), BF)], [], 1, tab, *near, name="pick_c"
    )
    near.append(swap(wanted, "c", 2, 1))
    (wanted,) = call(functools.partial(pick_body, FIRST + 36, 48), [EDGES], [], 1, tab, *near, name="pick_z")
    (mine,) = call(functools.partial(pick_body, FIRST, 48), [EDGES], [], 1, tab, *near, name="pick_own")
    return [mine, swap(wanted, "zl", 2, 1)]


def g_of(v):
    return v * lax.rsqrt(v * v + smooth_sq)


def shards(features, observed, conv_weights, head_weight, adjacency, placement_map):
    zl, y, c, zh, x = (lax.axis_index(n) for n in FACE + MEM)
    core = jnp.stack([c, zh, x, y, zl]).astype(jnp.int32)
    head_rows = jnp.pad(head_weight, ((0, 0), (0, 176)))
    mine = jnp.concatenate([conv_weights[:, 0], conv_weights[:, 1], head_rows], axis=0)
    mine = jnp.broadcast_to(mine[None], (64, 38, 256))
    coords = jnp.stack([zl, y, c]).astype(jnp.int32)
    coords, mine = lax.optimization_barrier((coords, mine))
    tab = make_table(adjacency, placement_map, coords)
    fields = features.reshape(6, 256, 256)
    (edges,) = call(edges_body, [EDGES], [], 0, fields, name="edges", us=2)
    near = [edges] + [swap(edges, "y", 4, k) for k in (1, 2, 3)]
    tab, mine, *near = lax.optimization_barrier((tab, mine, *near))
    mine = trade(mine, CORE)
    near = exchange_all(tab, near)
    obs = jnp.pad(jnp.swapaxes(observed, 1, 2), ((0, 0), (0, 0), (0, 48)))
    over = tab[72] > SLOTS
    mine, obs, over, *near = lax.optimization_barrier((mine, obs, over, *near))
    one, two = call(
        weights_body,
        [((8, 144, 256), BF), ((8, 160, 256), BF)],
        [((2, 160, 256), F32)],
        0,
        mine,
        name="weights",
    )
    one_too, two_too = swap(one, "c", 2, 1), swap(two, "c", 2, 1)
    args = (tab, core, fields, *near, one, one_too)
    edges, sent = call(
        sides_body,
        [EDGES, POST],
        [((384, 2304), BF), WEIGHT, *SHIFTS],
        2,
        *args,
        name="sides",
        us=7,
    )
    sent, two, two_too, obs = lax.optimization_barrier((sent, two, two_too, obs))
    got = trade(sent, ("zl", "y"))
    wide_in, pre_one, act_one = call(
        functools.partial(conv_body, False, True, 2),
        [WIDE, PRE, ACT],
        [WEIGHT, *SHIFTS],
        2,
        *args,
        name="conv_one",
        us=7,
    )
    got, wide_in, pre_one, act_one = lax.optimization_barrier((got, wide_in, pre_one, act_one))
    near = exchange(tab, over, edges, got)
    args = (tab, core, act_one, *near, two, two_too)
    (outputs,) = call(
        functools.partial(conv_body, True, False, 4),
        [((8, 6, 32, 128), BF)],
        [WIDE, PRE, WEIGHT, ((256, 128), BF), ACT, *SHIFTS],
        2,
        *args,
        name="conv_two",
        us=7,
    )
    vals = trade(outputs, MEM)
    wide_mid, pre_two, weight, head = call(
        functools.partial(conv_body, True, True, 4),
        [WIDE, PRE, WEIGHT, ((256, 128), BF)],
        SHIFTS,
        2,
        *args,
        name="keep_two",
        us=7,
    )
    vals, wide_mid, pre_two, weight, head = lax.optimization_barrier((vals, wide_mid, pre_two, weight, head))
    (slopes,) = call(score_body, [((8, 6, 32, 128), BF)], [], 0, vals, obs, name="score")
    slopes = trade(slopes, MEM)
    slope, head_grad, edges, sent = call(
        slope_body,
        [ACT, ((256, 128), F32), EDGES, POST],
        [((12, 96, 256), BF), ((6, 256, 128), BF), ((192, 256), BF), ACT],
        1,
        *(tab, slopes, head, pre_two, weight),
        name="slope",
        us=4,
    )
    got = trade(sent, ("zl", "y"))
    keep_two, give_two, inner = call(
        back_body,
        [((8, 8, 20, 256), F32), ((8, 8, 20, 256), F32), ACT],
        [((2304, 256), F32), ((3, 6, 288, 256), BF), ((576, 256), BF)],
        1,
        *(core, wide_mid, slope, head_grad, weight),
        name="back",
        us=6,
    )
    got, inner = lax.optimization_barrier((got, inner))
    near = exchange(tab, over, edges, got)
    got_two = swap(give_two, "c", 2, 1)
    keep_one, give_one = call(
        first_body,
        [((8, 144, 256), F32), ((8, 144, 256), F32)],
        [((6, 64, 256), BF), ((6, 256, 256), BF), ((2304, 256), F32)],
        2,
        *(tab, core, *near, inner, pre_one, wide_in),
        name="first",
        us=4,
    )
    got_one = swap(give_one, "c", 2, 1)
    (packed,) = call(
        pack_body, [((64, 38, 256), F32)], [], 0, keep_one, got_one, keep_two, got_two, name="pack"
    )
    return call(add_body, [((18, 2, 256), F32), ((2, 80), F32)], [], 0, trade(packed, CORE), name="add")


def solution(mesh):
    fine = Mesh(mesh.devices.reshape(2, 4, 2, 2, 4), FACE + MEM)
    both = FACE + MEM
    in_specs = (P(MEM, FACE), P(FACE, None, MEM), P(both), P(both), P(), P())
    return jax.shard_map(
        shards, mesh=fine, in_specs=in_specs, out_specs=(P(both), P(both)), check_vma=False
    )
```

```python
import functools

import jax
import jax.numpy as jnp
from jax import lax
from jax.experimental import pallas as pl
from jax.experimental.pallas import tpu as pltpu
from jax.sharding import Mesh
from jax.sharding import PartitionSpec as P

smooth_sq = 0.0625
BF = jnp.bfloat16
F32 = jnp.float32
FACE = ("zl", "y", "c")
MEM = ("zh", "x")
CORE = ("zl", "y", "zh", "x")
SLOTS = 6
FIRST = 80
LATE = 176
OWN = 200


def swap(value, axes, size, k):
    return lax.ppermute(value, axes, [(i, i ^ k) for i in range(size)])


def ones_in(v):
    v = v - ((v >> 1) & 0x5555)
    v = (v & 0x3333) + ((v >> 2) & 0x3333)
    v = (v + (v >> 4)) & 0x0F0F
    return (v + (v >> 8)) & 0x1F


def table_body(adj, placed, coords, tab, slot_of, marks, many):
    chip, c = coords[0] * 4 + coords[1], coords[2]
    me = chip * 2 + c

    def note(s, carry):
        slot_of[placed[s]] = s
        return carry

    lax.fori_loop(0, 48, note, 0)

    def clear(i, carry):
        marks[i] = 0
        many[i] = 0
        return carry

    lax.fori_loop(0, 128, clear, 0)

    def where_from(slot, side):
        base = (placed[slot] * 4 + side) * 3
        source = slot_of[adj[base]]
        face = (source * 171) >> 9
        return face, (source - 3 * face) * 4 + adj[base + 1], adj[base + 2]

    def mark(slot, most):
        face = (slot * 171) >> 9
        for side in range(4):
            goal, _, _ = where_from(slot, side)
            at = face * 8 + (goal >> 1)
            count = many[at] + 1
            many[at] = count
            marks[at] = marks[at] | (1 << ((slot - 3 * face) * 4 + side))
            most = jnp.where((goal >> 1) == (face >> 1), most, jnp.maximum(most, count))
        return most

    tab[72] = lax.fori_loop(0, 48, mark, 0)

    def one(i, carry):
        goal, _, flip = where_from(3 * me + (i >> 2), i & 3)
        rank = ones_in(marks[me * 8 + (goal >> 1)] & ((1 << i) - 1))
        tab[48 + i] = jnp.where((goal >> 1) == chip, 255, (goal >> 1) * 16 + rank)
        tab[60 + i] = flip
        for t, core in enumerate((c, 1 - c)):
            face, row, _ = where_from(3 * (chip * 2 + core) + (i >> 2), i & 3)
            rank = ones_in(marks[face * 8 + chip] & ((1 << row) - 1))
            local = (face >> 1) == chip
            other = (face & 1) != c
            late = jnp.logical_not(local | other) & (rank >= SLOTS)
            at = (face >> 1) * SLOTS + rank
            which = jnp.where(local, 0, jnp.where(late, 3, 1))
            row = jnp.where(local, row, jnp.where(late, 12 * t + i, at))
            tab[LATE + 12 * t + i] = jnp.where(late, at - SLOTS, -1)
            tab[24 * t + i] = jnp.where(other, 2 if t == 0 else 0, which)
            tab[24 * t + 12 + i] = jnp.where(other, i if t == 0 else 0, row)
        for t, (dz, dc) in enumerate(((0, 0), (0, 1), (1, 1), (1, 0))):
            slot = 3 * (((coords[0] ^ dz) * 4 + coords[1]) * 2 + (c ^ dc)) + (i >> 2)
            face, row, _ = where_from(slot, i & 3)
            which = ((face >> 1) & 3) ^ coords[1]
            other = (face & 1) != c
            if t == 0 or t == 3:
                which = jnp.where(other, 4, which)
                row = jnp.where(other, i if t == 0 else 12 + i, row)
            if t == 0:
                tab[OWN + i] = jnp.where((face >> 3) != coords[0], 1, 0)
                tab[OWN + 12 + i] = i
            tab[FIRST + t * 12 + i] = which
            tab[FIRST + 48 + t * 12 + i] = row
        return carry

    lax.fori_loop(0, 12, one, 0)


def make_table(adjacency, placement_map, coords):
    return pl.pallas_call(
        table_body,
        out_shape=jax.ShapeDtypeStruct((OWN + 24,), jnp.int32),
        in_specs=[pl.BlockSpec(memory_space=pltpu.SMEM)] * 3,
        out_specs=pl.BlockSpec(memory_space=pltpu.SMEM),
        scratch_shapes=[pltpu.SMEM((n,), jnp.int32) for n in (48, 128, 128)],
        name="table",
    )(adjacency.reshape(-1), placement_map, coords)


def post_edges(first, tab, edges, out):
    for i in range(12):
        code = tab[48 + i]
        rank = (code & 15) - first

        @pl.when((code != 255) & (rank >= 0) & (rank < SLOTS))
        def _():
            out[(code >> 4) * SLOTS + rank] = edges[i]


def late_body(tab, rest, out):
    for i in range(24):
        at = tab[LATE + i]

        @pl.when(at >= 0)
        def _():
            out[i] = rest[at]


def choose(tab, first, step, i, refs):
    which = tab[first + i]
    row = tab[first + step + i]
    got = refs[0][jnp.minimum(row, 11)]
    for n, ref in enumerate(refs[1:], 1):
        got = jnp.where(which == n, ref[jnp.minimum(row, ref.shape[0] - 1)], got)
    return got


def pick_body(first, step, tab, *refs):
    for i in range(refs[-1].shape[0]):
        refs[-1][i] = choose(tab, first, step, i, refs[:-1])


def rims_into(tab, first, step, refs, rim):
    r = lax.broadcasted_iota(jnp.int32, (32, 32), 0)
    q = lax.broadcasted_iota(jnp.int32, (32, 32), 1)
    for i in range(12):
        goal = jnp.where(tab[60 + i] == 1, (r & 16) + 15 - (r & 15), r)
        turn = (q == goal).astype(F32).astype(BF)
        line = dot(turn, choose(tab, first, step, i, refs)).astype(BF)
        for m in range(2):
            rim[(i // 4) * 2 + m, (i % 4) * 16 : (i % 4) * 16 + 16] = line[m * 16 : m * 16 + 16]


def dot(a, b, dims=((1,), (0,))):
    return lax.dot_general(a, b, (dims, ((), ())), preferred_element_type=F32)


def grid_of(rows, columns):
    return (
        lax.broadcasted_iota(jnp.int32, (rows, columns), 0),
        lax.broadcasted_iota(jnp.int32, (rows, columns), 1),
    )


def one_hot(mask):
    return mask.astype(F32).astype(BF)


def cell_of(side, k):
    return jnp.where(side == 0, k, jnp.where(side == 1, 16 * k + 15, jnp.where(side == 2, 240 + k, 16 * k)))


def select_rows(row, column):
    return one_hot(cell_of(row >> 4, row & 15) == column)


def line_rows():
    row, column = grid_of(192, 256)
    part = row >> 4
    side = (part * 11) >> 5
    k = (row & 15) + 1 - (part - 3 * side)
    return one_hot((k >= 0) & (k < 16) & (cell_of(side, k) == column))


def shift_rows(columns):
    row, column = grid_of(576, columns)
    n = jnp.where(row >= 288, 1, 0)
    r = row - 288 * n
    i = (r >> 4) - 1
    k = (r & 15) + 2 * n - 1
    inside = (k >= 0) & (k < 16)
    middle = (i >= 0) & (i < 16)
    if columns == 256:
        return one_hot(inside & middle & (column == 16 * i + k))
    ends = jnp.where(i < 0, k, 32 + k)
    sides = jnp.where(k < 0, 48 + i, 16 + i)
    outer = jnp.logical_not(middle) & inside & (column == ends)
    return one_hot(outer | (middle & jnp.logical_not(inside) & (column == sides)))


def edge_rows(columns):
    row, column = grid_of(576, columns)
    tap = row >> 6
    down = (tap * 11) >> 5
    cell = cell_of((row >> 4) & 3, row & 15)
    i = (cell >> 4) + down - 1
    j = (cell & 15) + tap - 3 * down - 1
    in_i, in_j = (i >= 0) & (i < 16), (j >= 0) & (j < 16)
    if columns == 256:
        return one_hot(in_i & in_j & (column == 16 * i + j))
    ends = in_j & jnp.logical_not(in_i) & (column == jnp.where(i < 0, j, 32 + j))
    sides = in_i & jnp.logical_not(in_j) & (column == jnp.where(j < 0, 48 + i, 16 + i))
    return one_hot(ends | sides)


def put_edges(t, edges, lines):
    m = t // 3
    s = t - 3 * m
    for side in range(4):
        edges[4 * s + side, pl.ds(pl.multiple_of(m * 16, 16), 16)] = lines[side * 16 : side * 16 + 16]


def sigmoid(v):
    return 1.0 / (1.0 + jnp.exp(-v))


def edges_body(x, edges):
    select = select_rows(*grid_of(64, 256))

    def tile(t, carry):
        put_edges(t, edges, dot(select, x[t]).astype(BF))
        return carry

    lax.fori_loop(0, 6, tile, 0, unroll=True)


def weights_body(mine, one, two, wide):
    for q in range(8):
        for r in range(8):
            block = mine[8 * q + r].astype(F32)
            wide[0, 18 * r : 18 * r + 18] = block[:18]
            wide[1, 18 * r : 18 * r + 18] = block[18:36]
            wide[1, 144 + 2 * r : 146 + 2 * r] = block[36:38]
        one[q] = wide[0, :144].astype(BF)
        two[q] = wide[1].astype(BF)


def fill_weight(core, own, other, weight):
    c = core[0]
    for q in range(8):
        for part, k in ((own, c), (other, 1 - c)):
            weight[pl.ds(pl.multiple_of((2 * q + k) * 144, 144), 144)] = part[q, :144]


def sides_body(tab, core, x, a, b, own, other, edges, sent, seen, weight, rim, rows_x, rows_r):
    rows_x[...] = edge_rows(256)
    rows_r[...] = edge_rows(64)
    fill_weight(core, own, other, weight)
    rims_into(tab, OWN, 12, (a, b), rim)
    for t in range(6):
        m, s = divmod(t, 3)
        part = (dot(rows_x[...], x[t]) + dot(rows_r[...], rim[s * 2 + m])).astype(BF)
        for tap in range(9):
            seen[64 * t : 64 * t + 64, 256 * tap : 256 * tap + 256] = part[64 * tap : 64 * tap + 64]
    v = dot(seen[...], weight[...])
    line = (v * sigmoid(v)).astype(BF)
    for t in range(6):
        m, s = divmod(t, 3)
        for side in range(4):
            at = 64 * t + 16 * side
            edges[4 * s + side, 16 * m : 16 * m + 16] = line[at : at + 16]
    post_edges(0, tab, edges, sent)


def conv_body(last, keep, count, tab, core, x, *refs):
    near, refs = refs[:count], refs[count:]
    own, other, *refs = refs
    *refs, rim, shift_x, shift_r = refs
    if last and keep:
        wide, pre, weight, head = refs
    elif last:
        out, wide, pre, weight, head, act = refs
    elif keep:
        wide, pre, act, weight = refs
    else:
        edges_out, sent, wide, pre, act, weight = refs
        select = select_rows(*grid_of(64, 256))
    shift_x[...] = shift_rows(256)
    shift_r[...] = shift_rows(64)
    c = core[0]
    for q in range(8):
        for part, k in ((own, c), (other, 1 - c)):
            at = pl.multiple_of((2 * q + k) * 144, 144)
            weight[pl.ds(at, 144)] = part[q, :144]
            if last:
                at = pl.multiple_of((2 * q + k) * 16, 16)
                head[pl.ds(at, 16)] = part[q, 144:160, :128]
    rims_into(tab, *((0, 12) if last else (OWN, 12)), near, rim)
    for t in range(6):
        m, s = divmod(t, 3)
        r = rim[s * 2 + m]
        v = x[t]
        wide[t, :16, 256:512] = r[:16]
        wide[t, 16:272, 256:512] = v
        wide[t, 272:, 256:512] = r[32:48]
        moved = (dot(shift_x[...], v) + dot(shift_r[...], r)).astype(BF)
        wide[t, :, :256] = moved[:288]
        wide[t, :, 512:] = moved[288:]
    total = dot(wide[:, :256].reshape(1536, 768), weight[:768])
    total += dot(wide[:, 16:272].reshape(1536, 768), weight[768:1536])
    total += dot(wide[:, 32:].reshape(1536, 768), weight[1536:])
    pre[...] = total.reshape(6, 256, 256)
    if last and keep:
        return
    for t in range(6):
        v = pre[t]
        act[t] = (v * sigmoid(v)).astype(BF)
        if not last and not keep:
            put_edges(t, edges_out, dot(select, act[t]).astype(BF))
    if not last and not keep:
        post_edges(0, tab, edges_out, sent)
    if last:
        o = dot(act[...].reshape(1536, 256), head[...]).astype(BF)
        for t in range(6):
            for q in range(8):
                out[q, t] = o[256 * t + 32 * q : 256 * t + 32 * q + 32]


def score_body(vals, obs, out):
    for s in range(3):
        for h in range(2):
            rows = slice(16 * h, 16 * h + 16)
            y = [vals[k // 2, (k % 2) * 3 + s, rows].astype(F32) for k in range(16)]
            o = obs[s, rows].astype(F32)
            paired = [jnp.zeros((16, 128), F32) for _ in range(16)]
            for a in range(16):
                for b in range(a + 1, 16):
                    g = g_of(y[a] - y[b])
                    paired[a] = paired[a] + g
                    paired[b] = paired[b] - g
            for k in range(16):
                value = (g_of(y[k] - o) / 16 - paired[k] / 256) / 16
                out[k // 2, (k % 2) * 3 + s, rows] = value.astype(BF)


def slope_body(tab, slopes, head, pre, weight, slope, head_grad, edges, sent, rows, cells, lines, act):
    lines[...] = line_rows()
    for t in range(6):
        for q in range(8):
            cells[t, 32 * q : 32 * q + 32] = slopes[q, t]
    out = cells[...].reshape(1536, 128)
    back = dot(out, head[...], ((1,), (1,)))
    for t in range(6):
        m, s = divmod(t, 3)
        v = pre[t]
        g = sigmoid(v)
        act[t] = (v * g).astype(BF)
        b = (back[256 * t : 256 * t + 256] * (g * (1.0 + v * (1.0 - g)))).astype(BF)
        slope[t] = b
        line = dot(lines[...], b).astype(BF)
        at = (s * 2 + m) * 16
        for k in range(12):
            rows[k, at : at + 16] = line[16 * k : 16 * k + 16]
    head_grad[...] = dot(act[...].reshape(1536, 256), out, ((0,), (0,)))
    for side, taps in enumerate(((0, 1, 2), (2, 5, 8), (6, 7, 8), (0, 3, 6))):
        total = sum(
            dot(rows[3 * side + t], weight[tap * 256 : tap * 256 + 256], ((1,), (1,)))
            for t, tap in enumerate(taps)
        ).astype(BF)
        for s in range(3):
            edges[4 * s + side] = total[32 * s : 32 * s + 32]
    post_edges(0, tab, edges, sent)


def grad_into(wide, slope, sums):
    flat = slope[...].reshape(1536, 256)
    for a in range(3):
        sums[768 * a : 768 * a + 768] = dot(
            wide[:, 16 * a : 16 * a + 256].reshape(1536, 768), flat, ((0,), (0,))
        )


def split_cores(c, sums, keep, give):
    for q in range(8):
        keep[q] = sums[pl.ds(pl.multiple_of((2 * q + c) * 144, 144), 144)]
        give[q] = sums[pl.ds(pl.multiple_of((2 * q + 1 - c) * 144, 144), 144)]


def back_body(core, wide, slope, head_grad, weight, keep, give, inner, sums, moved, shift_x):
    c = core[0]
    grad_into(wide, slope, sums)
    for q in range(8):
        for ref, k in ((keep, c), (give, 1 - c)):
            block = sums[pl.ds(pl.multiple_of((2 * q + k) * 144, 144), 144)]
            rows = head_grad[pl.ds(pl.multiple_of((2 * q + k) * 16, 16), 16)]
            for r in range(8):
                ref[r, q, :18] = block[18 * r : 18 * r + 18]
                ref[r, q, 18:20, :128] = rows[2 * r : 2 * r + 2]
                ref[r, q, 18:20, 128:] = jnp.zeros((2, 128), F32)

    shift_x[...] = shift_rows(256)
    for t in range(6):
        v = slope[t]
        moved[1, t, :16] = jnp.zeros((16, 256), BF)
        moved[1, t, 16:272] = v
        moved[1, t, 272:] = jnp.zeros((16, 256), BF)
        both = dot(shift_x[...], v).astype(BF)
        moved[0, t] = both[:288]
        moved[2, t] = both[288:]
    total = None
    for tap in range(9):
        a, b = tap // 3, tap % 3
        part = dot(
            moved[2 - b, :, 16 * (2 - a) : 16 * (2 - a) + 256].reshape(1536, 256),
            weight[tap * 256 : tap * 256 + 256],
            ((1,), (1,)),
        )
        total = part if total is None else total + part
    inner[...] = total.astype(BF).reshape(6, 256, 256)


def first_body(tab, core, edges, got, cores, late, inner, pre, wide, keep, give, rim, slope, sums):
    column, row = grid_of(256, 64)
    spread = select_rows(row, column)
    rims_into(tab, 0, 12, (edges, got, cores, late), rim)

    def tile(t, carry):
        m = t // 3
        s = t - 3 * m
        mid = inner[t].astype(F32) + dot(spread, rim[s * 2 + m])
        v = pre[t]
        g = sigmoid(v)
        slope[t] = (mid * (g * (1.0 + v * (1.0 - g)))).astype(BF)
        return carry

    lax.fori_loop(0, 6, tile, 0, unroll=True)
    grad_into(wide, slope, sums)
    split_cores(core[0], sums, keep, give)


def pack_body(keep, got, keep_two, got_two, out):
    for q in range(8):
        one = keep[q] + got[q]
        for r in range(8):
            out[8 * q + r, :18] = one[18 * r : 18 * r + 18]
            out[8 * q + r, 18:38] = keep_two[r, q] + got_two[r, q]


def add_body(parts, out, last):
    total = parts[0]
    for k in range(1, 64):
        total = total + parts[k]
    out[:, 0, :] = total[:18]
    out[:, 1, :] = total[18:36]
    last[...] = total[36:38, :80]


def call(body, outs, scratch, scalars, *args, name, us=1):
    vmem = pl.BlockSpec(memory_space=pltpu.VMEM)
    return pl.pallas_call(
        body,
        out_shape=[jax.ShapeDtypeStruct(shape, kind) for shape, kind in outs],
        in_specs=[pl.BlockSpec(memory_space=pltpu.SMEM)] * scalars + [vmem] * (len(args) - scalars),
        out_specs=[vmem] * len(outs),
        scratch_shapes=[pltpu.VMEM(shape, kind) for shape, kind in scratch],
        compiler_params=pltpu.CompilerParams(vmem_limit_bytes=16 << 20),
        cost_estimate=pl.CostEstimate(flops=us * 1000000000, bytes_accessed=1000, transcendentals=0),
        name=name,
    )(*args)


def trade(value, axes):
    return lax.all_to_all(value, axes, split_axis=0, concat_axis=0, tiled=True)


EDGES = ((12, 32, 256), BF)
WIDE = ((6, 288, 768), BF)
PRE = ((6, 256, 256), F32)
ACT = ((6, 256, 256), BF)


WEIGHT = ((2304, 256), BF)
SHIFTS = [((6, 64, 256), BF), ((576, 256), BF), ((576, 64), BF)]
POST = ((8 * SLOTS, 32, 256), BF)
SLOTS_LATE = ((24, 32, 256), BF)


def later(tab, edges):
    (sent,) = call(functools.partial(post_edges, SLOTS), [POST], [], 1, tab, edges, name="post_late")
    return call(late_body, [SLOTS_LATE], [], 1, tab, trade(sent, ("zl", "y")), name="late")[0]


def exchange(tab, over, edges, got):
    late = lax.cond(
        over, lambda e: later(tab, e), lambda e: jnp.zeros((24, 32, 256), BF), edges
    )
    refs = (edges, got, edges, late)
    (wanted,) = call(functools.partial(pick_body, 24, 12), [EDGES], [], 1, tab, *refs, name="pick")
    return edges, got, swap(wanted, "c", 2, 1), late


def exchange_all(tab, near):
    (wanted,) = call(
        functools.partial(pick_body, FIRST + 12, 48), [((24, 32, 256), BF)], [], 1, tab, *near, name="pick_c"
    )
    near.append(swap(wanted, "c", 2, 1))
    (wanted,) = call(functools.partial(pick_body, FIRST + 36, 48), [EDGES], [], 1, tab, *near, name="pick_z")
    (mine,) = call(functools.partial(pick_body, FIRST, 48), [EDGES], [], 1, tab, *near, name="pick_own")
    return [mine, swap(wanted, "zl", 2, 1)]


def g_of(v):
    return v * lax.rsqrt(v * v + smooth_sq)


def shards(features, observed, conv_weights, head_weight, adjacency, placement_map):
    zl, y, c, zh, x = (lax.axis_index(n) for n in FACE + MEM)
    core = jnp.stack([c, zh, x, y, zl]).astype(jnp.int32)
    head_rows = jnp.pad(head_weight, ((0, 0), (0, 176)))
    mine = jnp.concatenate([conv_weights[:, 0], conv_weights[:, 1], head_rows], axis=0)
    mine = jnp.broadcast_to(mine[None], (64, 38, 256))
    coords = jnp.stack([zl, y, c]).astype(jnp.int32)
    coords, mine = lax.optimization_barrier((coords, mine))
    tab = make_table(adjacency, placement_map, coords)
    fields = features.reshape(6, 256, 256)
    (edges,) = call(edges_body, [EDGES], [], 0, fields, name="edges", us=2)
    near = [edges] + [swap(edges, "y", 4, k) for k in (1, 2, 3)]
    tab, mine, *near = lax.optimization_barrier((tab, mine, *near))
    mine = trade(mine, CORE)
    near = exchange_all(tab, near)
    obs = jnp.pad(jnp.swapaxes(observed, 1, 2), ((0, 0), (0, 0), (0, 48)))
    over = tab[72] > SLOTS
    mine, obs, over, *near = lax.optimization_barrier((mine, obs, over, *near))
    one, two = call(
        weights_body,
        [((8, 144, 256), BF), ((8, 160, 256), BF)],
        [((2, 160, 256), F32)],
        0,
        mine,
        name="weights",
    )
    one_too = swap(one, "c", 2, 1)
    args = (tab, core, fields, *near, one, one_too)
    edges, sent = call(
        sides_body,
        [EDGES, POST],
        [((384, 2304), BF), WEIGHT, *SHIFTS],
        2,
        *args,
        name="sides",
        us=7,
    )
    sent, two, obs = lax.optimization_barrier((sent, two, obs))
    got = trade(sent, ("zl", "y"))
    two_too = swap(two, "c", 2, 1)
    wide_in, pre_one, act_one = call(
        functools.partial(conv_body, False, True, 2),
        [WIDE, PRE, ACT],
        [WEIGHT, *SHIFTS],
        2,
        *args,
        name="conv_one",
        us=7,
    )
    got, two_too, wide_in, pre_one, act_one = lax.optimization_barrier((got, two_too, wide_in, pre_one, act_one))
    near = exchange(tab, over, edges, got)
    args = (tab, core, act_one, *near, two, two_too)
    (outputs,) = call(
        functools.partial(conv_body, True, False, 4),
        [((8, 6, 32, 128), BF)],
        [WIDE, PRE, WEIGHT, ((256, 128), BF), ACT, *SHIFTS],
        2,
        *args,
        name="conv_two",
        us=7,
    )
    vals = trade(outputs, MEM)
    wide_mid, pre_two, weight, head = call(
        functools.partial(conv_body, True, True, 4),
        [WIDE, PRE, WEIGHT, ((256, 128), BF)],
        SHIFTS,
        2,
        *args,
        name="keep_two",
        us=7,
    )
    vals, wide_mid, pre_two, weight, head = lax.optimization_barrier((vals, wide_mid, pre_two, weight, head))
    (slopes,) = call(score_body, [((8, 6, 32, 128), BF)], [], 0, vals, obs, name="score")
    slopes = trade(slopes, MEM)
    slope, head_grad, edges, sent = call(
        slope_body,
        [ACT, ((256, 128), F32), EDGES, POST],
        [((12, 96, 256), BF), ((6, 256, 128), BF), ((192, 256), BF), ACT],
        1,
        *(tab, slopes, head, pre_two, weight),
        name="slope",
        us=4,
    )
    got = trade(sent, ("zl", "y"))
    keep_two, give_two, inner = call(
        back_body,
        [((8, 8, 20, 256), F32), ((8, 8, 20, 256), F32), ACT],
        [((2304, 256), F32), ((3, 6, 288, 256), BF), ((576, 256), BF)],
        1,
        *(core, wide_mid, slope, head_grad, weight),
        name="back",
        us=6,
    )
    got, inner = lax.optimization_barrier((got, inner))
    near = exchange(tab, over, edges, got)
    got_two = swap(give_two, "c", 2, 1)
    keep_one, give_one = call(
        first_body,
        [((8, 144, 256), F32), ((8, 144, 256), F32)],
        [((6, 64, 256), BF), ((6, 256, 256), BF), ((2304, 256), F32)],
        2,
        *(tab, core, *near, inner, pre_one, wide_in),
        name="first",
        us=4,
    )
    got_one = swap(give_one, "c", 2, 1)
    (packed,) = call(
        pack_body, [((64, 38, 256), F32)], [], 0, keep_one, got_one, keep_two, got_two, name="pack"
    )
    return call(add_body, [((18, 2, 256), F32), ((2, 80), F32)], [], 0, trade(packed, CORE), name="add")


def solution(mesh):
    fine = Mesh(mesh.devices.reshape(2, 4, 2, 2, 4), FACE + MEM)
    both = FACE + MEM
    in_specs = (P(MEM, FACE), P(FACE, None, MEM), P(both), P(both), P(), P())
    return jax.shard_map(
        shards, mesh=fine, in_specs=in_specs, out_specs=(P(both), P(both)), check_vma=False
    )
```

```python
import functools

import jax
import jax.numpy as jnp
from jax import lax
from jax.experimental import pallas as pl
from jax.experimental.pallas import tpu as pltpu
from jax.sharding import Mesh
from jax.sharding import PartitionSpec as P

smooth_sq = 0.0625
BF = jnp.bfloat16
F32 = jnp.float32
FACE = ("zl", "y", "c")
MEM = ("zh", "x")
CORE = ("zl", "y", "zh", "x")
SLOTS = 6
FIRST = 80
LATE = 176
OWN = 200


def swap(value, axes, size, k):
    return lax.ppermute(value, axes, [(i, i ^ k) for i in range(size)])


def ones_in(v):
    v = v - ((v >> 1) & 0x5555)
    v = (v & 0x3333) + ((v >> 2) & 0x3333)
    v = (v + (v >> 4)) & 0x0F0F
    return (v + (v >> 8)) & 0x1F


def table_body(adj, placed, coords, tab, slot_of, marks, many):
    chip, c = coords[0] * 4 + coords[1], coords[2]
    me = chip * 2 + c

    def note(s, carry):
        slot_of[placed[s]] = s
        return carry

    lax.fori_loop(0, 48, note, 0)

    def clear(i, carry):
        marks[i] = 0
        many[i] = 0
        return carry

    lax.fori_loop(0, 128, clear, 0)

    def where_from(slot, side):
        base = (placed[slot] * 4 + side) * 3
        source = slot_of[adj[base]]
        face = (source * 171) >> 9
        return face, (source - 3 * face) * 4 + adj[base + 1], adj[base + 2]

    def mark(slot, most):
        face = (slot * 171) >> 9
        for side in range(4):
            goal, _, _ = where_from(slot, side)
            at = face * 8 + (goal >> 1)
            count = many[at] + 1
            many[at] = count
            marks[at] = marks[at] | (1 << ((slot - 3 * face) * 4 + side))
            most = jnp.where((goal >> 1) == (face >> 1), most, jnp.maximum(most, count))
        return most

    tab[72] = lax.fori_loop(0, 48, mark, 0)

    def one(i, carry):
        goal, _, flip = where_from(3 * me + (i >> 2), i & 3)
        rank = ones_in(marks[me * 8 + (goal >> 1)] & ((1 << i) - 1))
        tab[48 + i] = jnp.where((goal >> 1) == chip, 255, (goal >> 1) * 16 + rank)
        tab[60 + i] = flip
        for t, core in enumerate((c, 1 - c)):
            face, row, _ = where_from(3 * (chip * 2 + core) + (i >> 2), i & 3)
            rank = ones_in(marks[face * 8 + chip] & ((1 << row) - 1))
            local = (face >> 1) == chip
            other = (face & 1) != c
            late = jnp.logical_not(local | other) & (rank >= SLOTS)
            at = (face >> 1) * SLOTS + rank
            which = jnp.where(local, 0, jnp.where(late, 3, 1))
            row = jnp.where(local, row, jnp.where(late, 12 * t + i, at))
            tab[LATE + 12 * t + i] = jnp.where(late, at - SLOTS, -1)
            tab[24 * t + i] = jnp.where(other, 2 if t == 0 else 0, which)
            tab[24 * t + 12 + i] = jnp.where(other, i if t == 0 else 0, row)
        for t, (dz, dc) in enumerate(((0, 0), (0, 1), (1, 1), (1, 0))):
            slot = 3 * (((coords[0] ^ dz) * 4 + coords[1]) * 2 + (c ^ dc)) + (i >> 2)
            face, row, _ = where_from(slot, i & 3)
            which = ((face >> 1) & 3) ^ coords[1]
            other = (face & 1) != c
            if t == 0 or t == 3:
                which = jnp.where(other, 4, which)
                row = jnp.where(other, i if t == 0 else 12 + i, row)
            if t == 0:
                tab[OWN + i] = jnp.where((face >> 3) != coords[0], 1, 0)
                tab[OWN + 12 + i] = i
            tab[FIRST + t * 12 + i] = which
            tab[FIRST + 48 + t * 12 + i] = row
        return carry

    lax.fori_loop(0, 12, one, 0)


def make_table(adjacency, placement_map, coords):
    return pl.pallas_call(
        table_body,
        out_shape=jax.ShapeDtypeStruct((OWN + 24,), jnp.int32),
        in_specs=[pl.BlockSpec(memory_space=pltpu.SMEM)] * 3,
        out_specs=pl.BlockSpec(memory_space=pltpu.SMEM),
        scratch_shapes=[pltpu.SMEM((n,), jnp.int32) for n in (48, 128, 128)],
        name="table",
    )(adjacency.reshape(-1), placement_map, coords)


def post_edges(first, tab, edges, out):
    for i in range(12):
        code = tab[48 + i]
        rank = (code & 15) - first

        @pl.when((code != 255) & (rank >= 0) & (rank < SLOTS))
        def _():
            out[(code >> 4) * SLOTS + rank] = edges[i]


def late_body(tab, rest, out):
    for i in range(24):
        at = tab[LATE + i]

        @pl.when(at >= 0)
        def _():
            out[i] = rest[at]


def choose(tab, first, step, i, refs):
    which = tab[first + i]
    row = tab[first + step + i]
    got = refs[0][jnp.minimum(row, 11)]
    for n, ref in enumerate(refs[1:], 1):
        got = jnp.where(which == n, ref[jnp.minimum(row, ref.shape[0] - 1)], got)
    return got


def pick_body(first, step, tab, *refs):
    for i in range(refs[-1].shape[0]):
        refs[-1][i] = choose(tab, first, step, i, refs[:-1])


def rims_into(tab, first, step, refs, rim):
    r = lax.broadcasted_iota(jnp.int32, (32, 32), 0)
    q = lax.broadcasted_iota(jnp.int32, (32, 32), 1)
    for i in range(12):
        goal = jnp.where(tab[60 + i] == 1, (r & 16) + 15 - (r & 15), r)
        turn = (q == goal).astype(F32).astype(BF)
        line = dot(turn, choose(tab, first, step, i, refs)).astype(BF)
        for m in range(2):
            rim[(i // 4) * 2 + m, (i % 4) * 16 : (i % 4) * 16 + 16] = line[m * 16 : m * 16 + 16]


def dot(a, b, dims=((1,), (0,))):
    return lax.dot_general(a, b, (dims, ((), ())), preferred_element_type=F32)


def grid_of(rows, columns):
    return (
        lax.broadcasted_iota(jnp.int32, (rows, columns), 0),
        lax.broadcasted_iota(jnp.int32, (rows, columns), 1),
    )


def one_hot(mask):
    return mask.astype(F32).astype(BF)


def cell_of(side, k):
    return jnp.where(side == 0, k, jnp.where(side == 1, 16 * k + 15, jnp.where(side == 2, 240 + k, 16 * k)))


def select_rows(row, column):
    return one_hot(cell_of(row >> 4, row & 15) == column)


def line_rows():
    row, column = grid_of(192, 256)
    part = row >> 4
    side = (part * 11) >> 5
    k = (row & 15) + 1 - (part - 3 * side)
    return one_hot((k >= 0) & (k < 16) & (cell_of(side, k) == column))


def shift_rows(columns):
    row, column = grid_of(576, columns)
    n = jnp.where(row >= 288, 1, 0)
    r = row - 288 * n
    i = (r >> 4) - 1
    k = (r & 15) + 2 * n - 1
    inside = (k >= 0) & (k < 16)
    middle = (i >= 0) & (i < 16)
    if columns == 256:
        return one_hot(inside & middle & (column == 16 * i + k))
    ends = jnp.where(i < 0, k, 32 + k)
    sides = jnp.where(k < 0, 48 + i, 16 + i)
    outer = jnp.logical_not(middle) & inside & (column == ends)
    return one_hot(outer | (middle & jnp.logical_not(inside) & (column == sides)))


def edge_rows(columns):
    row, column = grid_of(576, columns)
    tap = row >> 6
    down = (tap * 11) >> 5
    cell = cell_of((row >> 4) & 3, row & 15)
    i = (cell >> 4) + down - 1
    j = (cell & 15) + tap - 3 * down - 1
    in_i, in_j = (i >= 0) & (i < 16), (j >= 0) & (j < 16)
    if columns == 256:
        return one_hot(in_i & in_j & (column == 16 * i + j))
    ends = in_j & jnp.logical_not(in_i) & (column == jnp.where(i < 0, j, 32 + j))
    sides = in_i & jnp.logical_not(in_j) & (column == jnp.where(j < 0, 48 + i, 16 + i))
    return one_hot(ends | sides)


def put_edges(t, edges, lines):
    m = t // 3
    s = t - 3 * m
    for side in range(4):
        edges[4 * s + side, pl.ds(pl.multiple_of(m * 16, 16), 16)] = lines[side * 16 : side * 16 + 16]


def sigmoid(v):
    return 1.0 / (1.0 + jnp.exp(-v))


def edges_body(x, edges):
    select = select_rows(*grid_of(64, 256))

    def tile(t, carry):
        put_edges(t, edges, dot(select, x[t]).astype(BF))
        return carry

    lax.fori_loop(0, 6, tile, 0, unroll=True)


def weights_body(mine, one, two, wide):
    for q in range(8):
        for r in range(8):
            block = mine[8 * q + r].astype(F32)
            wide[0, 18 * r : 18 * r + 18] = block[:18]
            wide[1, 18 * r : 18 * r + 18] = block[18:36]
            wide[1, 144 + 2 * r : 146 + 2 * r] = block[36:38]
        one[q] = wide[0, :144].astype(BF)
        two[q] = wide[1].astype(BF)


def fill_weight(core, own, other, weight):
    c = core[0]
    for q in range(8):
        for part, k in ((own, c), (other, 1 - c)):
            weight[pl.ds(pl.multiple_of((2 * q + k) * 144, 144), 144)] = part[q, :144]


def sides_body(tab, core, x, a, b, own, other, edges, sent, seen, weight, rim, rows_x, rows_r):
    rows_x[...] = edge_rows(256)
    rows_r[...] = edge_rows(64)
    fill_weight(core, own, other, weight)
    rims_into(tab, OWN, 12, (a, b), rim)
    for t in range(6):
        m, s = divmod(t, 3)
        part = (dot(rows_x[...], x[t]) + dot(rows_r[...], rim[s * 2 + m])).astype(BF)
        for tap in range(9):
            seen[64 * t : 64 * t + 64, 256 * tap : 256 * tap + 256] = part[64 * tap : 64 * tap + 64]
    v = dot(seen[...], weight[...])
    line = (v * sigmoid(v)).astype(BF)
    for t in range(6):
        m, s = divmod(t, 3)
        for side in range(4):
            at = 64 * t + 16 * side
            edges[4 * s + side, 16 * m : 16 * m + 16] = line[at : at + 16]
    post_edges(0, tab, edges, sent)


def conv_body(last, keep, count, tab, core, x, *refs):
    near, refs = refs[:count], refs[count:]
    own, other, *refs = refs
    *refs, rim, shift_x, shift_r = refs
    if last and keep:
        wide, pre, weight, head = refs
    elif last:
        out, wide, pre, weight, head, act = refs
    elif keep:
        wide, pre, act, weight = refs
    else:
        edges_out, sent, wide, pre, act, weight = refs
        select = select_rows(*grid_of(64, 256))
    shift_x[...] = shift_rows(256)
    shift_r[...] = shift_rows(64)
    c = core[0]
    for q in range(8):
        for part, k in ((own, c), (other, 1 - c)):
            at = pl.multiple_of((2 * q + k) * 144, 144)
            weight[pl.ds(at, 144)] = part[q, :144]
            if last:
                at = pl.multiple_of((2 * q + k) * 16, 16)
                head[pl.ds(at, 16)] = part[q, 144:160, :128]
    rims_into(tab, *((0, 12) if last else (OWN, 12)), near, rim)
    for t in range(6):
        m, s = divmod(t, 3)
        r = rim[s * 2 + m]
        v = x[t]
        wide[t, :16, 256:512] = r[:16]
        wide[t, 16:272, 256:512] = v
        wide[t, 272:, 256:512] = r[32:48]
        moved = (dot(shift_x[...], v) + dot(shift_r[...], r)).astype(BF)
        wide[t, :, :256] = moved[:288]
        wide[t, :, 512:] = moved[288:]
    total = dot(wide[:, :256].reshape(1536, 768), weight[:768])
    total += dot(wide[:, 16:272].reshape(1536, 768), weight[768:1536])
    total += dot(wide[:, 32:].reshape(1536, 768), weight[1536:])
    pre[...] = total.reshape(6, 256, 256)
    if last and keep:
        return
    for t in range(6):
        v = pre[t]
        act[t] = (v * sigmoid(v)).astype(BF)
        if not last and not keep:
            put_edges(t, edges_out, dot(select, act[t]).astype(BF))
    if not last and not keep:
        post_edges(0, tab, edges_out, sent)
    if last:
        o = dot(act[...].reshape(1536, 256), head[...]).astype(BF)
        for t in range(6):
            for q in range(8):
                out[q, t] = o[256 * t + 32 * q : 256 * t + 32 * q + 32]


def score_body(vals, obs, out):
    for s in range(3):
        for h in range(2):
            rows = slice(16 * h, 16 * h + 16)
            y = [vals[k // 2, (k % 2) * 3 + s, rows].astype(F32) for k in range(16)]
            o = obs[s, rows].astype(F32)
            paired = [jnp.zeros((16, 128), F32) for _ in range(16)]
            for a in range(16):
                for b in range(a + 1, 16):
                    g = g_of(y[a] - y[b])
                    paired[a] = paired[a] + g
                    paired[b] = paired[b] - g
            for k in range(16):
                value = (g_of(y[k] - o) / 16 - paired[k] / 256) / 16
                out[k // 2, (k % 2) * 3 + s, rows] = value.astype(BF)


def slope_body(tab, slopes, head, pre, weight, slope, head_grad, edges, sent, rows, cells, lines, act):
    lines[...] = line_rows()
    for t in range(6):
        for q in range(8):
            cells[t, 32 * q : 32 * q + 32] = slopes[q, t]
    out = cells[...].reshape(1536, 128)
    back = dot(out, head[...], ((1,), (1,)))
    for t in range(6):
        m, s = divmod(t, 3)
        v = pre[t]
        g = sigmoid(v)
        act[t] = (v * g).astype(BF)
        b = (back[256 * t : 256 * t + 256] * (g * (1.0 + v * (1.0 - g)))).astype(BF)
        slope[t] = b
        line = dot(lines[...], b).astype(BF)
        at = (s * 2 + m) * 16
        for k in range(12):
            rows[k, at : at + 16] = line[16 * k : 16 * k + 16]
    head_grad[...] = dot(act[...].reshape(1536, 256), out, ((0,), (0,)))
    for side, taps in enumerate(((0, 1, 2), (2, 5, 8), (6, 7, 8), (0, 3, 6))):
        total = sum(
            dot(rows[3 * side + t], weight[tap * 256 : tap * 256 + 256], ((1,), (1,)))
            for t, tap in enumerate(taps)
        ).astype(BF)
        for s in range(3):
            edges[4 * s + side] = total[32 * s : 32 * s + 32]
    post_edges(0, tab, edges, sent)


def grad_into(wide, slope, sums):
    flat = slope[...].reshape(1536, 256)
    for a in range(3):
        sums[768 * a : 768 * a + 768] = dot(
            wide[:, 16 * a : 16 * a + 256].reshape(1536, 768), flat, ((0,), (0,))
        )


def split_cores(c, sums, keep, give):
    for q in range(8):
        keep[q] = sums[pl.ds(pl.multiple_of((2 * q + c) * 144, 144), 144)]
        give[q] = sums[pl.ds(pl.multiple_of((2 * q + 1 - c) * 144, 144), 144)]


def back_body(core, wide, slope, head_grad, weight, keep, give, inner, sums, moved, shift_x):
    c = core[0]
    grad_into(wide, slope, sums)
    for q in range(8):
        for ref, k in ((keep, c), (give, 1 - c)):
            block = sums[pl.ds(pl.multiple_of((2 * q + k) * 144, 144), 144)]
            rows = head_grad[pl.ds(pl.multiple_of((2 * q + k) * 16, 16), 16)]
            for r in range(8):
                ref[r, q, :18] = block[18 * r : 18 * r + 18]
                ref[r, q, 18:20, :128] = rows[2 * r : 2 * r + 2]
                ref[r, q, 18:20, 128:] = jnp.zeros((2, 128), F32)

    shift_x[...] = shift_rows(256)
    for t in range(6):
        v = slope[t]
        moved[1, t, :16] = jnp.zeros((16, 256), BF)
        moved[1, t, 16:272] = v
        moved[1, t, 272:] = jnp.zeros((16, 256), BF)
        both = dot(shift_x[...], v).astype(BF)
        moved[0, t] = both[:288]
        moved[2, t] = both[288:]
    total = None
    for tap in range(9):
        a, b = tap // 3, tap % 3
        part = dot(
            moved[2 - b, :, 16 * (2 - a) : 16 * (2 - a) + 256].reshape(1536, 256),
            weight[tap * 256 : tap * 256 + 256],
            ((1,), (1,)),
        )
        total = part if total is None else total + part
    inner[...] = total.astype(BF).reshape(6, 256, 256)


def first_body(tab, core, edges, got, cores, late, inner, pre, wide, keep, give, rim, slope, sums):
    column, row = grid_of(256, 64)
    spread = select_rows(row, column)
    rims_into(tab, 0, 12, (edges, got, cores, late), rim)

    def tile(t, carry):
        m = t // 3
        s = t - 3 * m
        mid = inner[t].astype(F32) + dot(spread, rim[s * 2 + m])
        v = pre[t]
        g = sigmoid(v)
        slope[t] = (mid * (g * (1.0 + v * (1.0 - g)))).astype(BF)
        return carry

    lax.fori_loop(0, 6, tile, 0, unroll=True)
    grad_into(wide, slope, sums)
    split_cores(core[0], sums, keep, give)


def pack_body(keep, got, keep_two, got_two, out):
    for q in range(8):
        one = keep[q] + got[q]
        for r in range(8):
            out[8 * q + r, :18] = one[18 * r : 18 * r + 18]
            out[8 * q + r, 18:38] = keep_two[r, q] + got_two[r, q]


def add_body(parts, out, last):
    total = parts[0]
    for k in range(1, 64):
        total = total + parts[k]
    out[:, 0, :] = total[:18]
    out[:, 1, :] = total[18:36]
    last[...] = total[36:38, :80]


def call(body, outs, scratch, scalars, *args, name, us=1):
    vmem = pl.BlockSpec(memory_space=pltpu.VMEM)
    return pl.pallas_call(
        body,
        out_shape=[jax.ShapeDtypeStruct(shape, kind) for shape, kind in outs],
        in_specs=[pl.BlockSpec(memory_space=pltpu.SMEM)] * scalars + [vmem] * (len(args) - scalars),
        out_specs=[vmem] * len(outs),
        scratch_shapes=[pltpu.VMEM(shape, kind) for shape, kind in scratch],
        compiler_params=pltpu.CompilerParams(vmem_limit_bytes=16 << 20),
        cost_estimate=pl.CostEstimate(flops=us * 1000000000, bytes_accessed=1000, transcendentals=0),
        name=name,
    )(*args)


def trade(value, axes):
    return lax.all_to_all(value, axes, split_axis=0, concat_axis=0, tiled=True)


EDGES = ((12, 32, 256), BF)
WIDE = ((6, 288, 768), BF)
PRE = ((6, 256, 256), F32)
ACT = ((6, 256, 256), BF)


WEIGHT = ((2304, 256), BF)
SHIFTS = [((6, 64, 256), BF), ((576, 256), BF), ((576, 64), BF)]
POST = ((8 * SLOTS, 32, 256), BF)
SLOTS_LATE = ((24, 32, 256), BF)


def later(tab, edges):
    (sent,) = call(functools.partial(post_edges, SLOTS), [POST], [], 1, tab, edges, name="post_late")
    return call(late_body, [SLOTS_LATE], [], 1, tab, trade(sent, ("zl", "y")), name="late")[0]


def exchange(tab, over, edges, got):
    late = lax.cond(
        over, lambda e: later(tab, e), lambda e: jnp.zeros((24, 32, 256), BF), edges
    )
    refs = (edges, got, edges, late)
    (wanted,) = call(functools.partial(pick_body, 24, 12), [EDGES], [], 1, tab, *refs, name="pick")
    return edges, got, swap(wanted, "c", 2, 1), late


def exchange_all(tab, near):
    (wanted,) = call(
        functools.partial(pick_body, FIRST + 12, 48), [((24, 32, 256), BF)], [], 1, tab, *near, name="pick_c"
    )
    near.append(swap(wanted, "c", 2, 1))
    (wanted,) = call(functools.partial(pick_body, FIRST + 36, 48), [EDGES], [], 1, tab, *near, name="pick_z")
    (mine,) = call(functools.partial(pick_body, FIRST, 48), [EDGES], [], 1, tab, *near, name="pick_own")
    return [mine, swap(wanted, "zl", 2, 1)]


def g_of(v):
    return v * lax.rsqrt(v * v + smooth_sq)


def shards(features, observed, conv_weights, head_weight, adjacency, placement_map):
    zl, y, c, zh, x = (lax.axis_index(n) for n in FACE + MEM)
    core = jnp.stack([c, zh, x, y, zl]).astype(jnp.int32)
    head_rows = jnp.pad(head_weight, ((0, 0), (0, 176)))
    mine = jnp.concatenate([conv_weights[:, 0], conv_weights[:, 1], head_rows], axis=0)
    mine = jnp.broadcast_to(mine[None], (64, 38, 256))
    coords = jnp.stack([zl, y, c]).astype(jnp.int32)
    coords, mine = lax.optimization_barrier((coords, mine))
    tab = make_table(adjacency, placement_map, coords)
    fields = features.reshape(6, 256, 256)
    (edges,) = call(edges_body, [EDGES], [], 0, fields, name="edges", us=2)
    near = [edges] + [swap(edges, "y", 4, k) for k in (1, 2, 3)]
    tab, mine, *near = lax.optimization_barrier((tab, mine, *near))
    mine = trade(mine, CORE)
    near = exchange_all(tab, near)
    obs = jnp.pad(jnp.swapaxes(observed, 1, 2), ((0, 0), (0, 0), (0, 48)))
    over = tab[72] > SLOTS
    mine, obs, over, *near = lax.optimization_barrier((mine, obs, over, *near))
    one, two = call(
        weights_body,
        [((8, 144, 256), BF), ((8, 160, 256), BF)],
        [((2, 160, 256), F32)],
        0,
        mine,
        name="weights",
    )
    one_too = swap(one, "c", 2, 1)
    args = (tab, core, fields, *near, one, one_too)
    edges, sent = call(
        sides_body,
        [EDGES, POST],
        [((384, 2304), BF), WEIGHT, *SHIFTS],
        2,
        *args,
        name="sides",
        us=7,
    )
    sent, two, obs = lax.optimization_barrier((sent, two, obs))
    got = trade(sent, ("zl", "y"))
    two_too = swap(two, "c", 2, 1)
    wide_in, pre_one, act_one = call(
        functools.partial(conv_body, False, True, 2),
        [WIDE, PRE, ACT],
        [WEIGHT, *SHIFTS],
        2,
        *args,
        name="conv_one",
        us=7,
    )
    got, two_too, wide_in, pre_one, act_one = lax.optimization_barrier((got, two_too, wide_in, pre_one, act_one))
    near = exchange(tab, over, edges, got)
    args = (tab, core, act_one, *near, two, two_too)
    (outputs,) = call(
        functools.partial(conv_body, True, False, 4),
        [((8, 6, 32, 128), BF)],
        [WIDE, PRE, WEIGHT, ((256, 128), BF), ACT, *SHIFTS],
        2,
        *args,
        name="conv_two",
        us=7,
    )
    vals = trade(outputs, MEM)
    wide_mid, pre_two, weight, head = call(
        functools.partial(conv_body, True, True, 4),
        [WIDE, PRE, WEIGHT, ((256, 128), BF)],
        SHIFTS,
        2,
        *args,
        name="keep_two",
        us=7,
    )
    vals, wide_mid, pre_two, weight, head = lax.optimization_barrier((vals, wide_mid, pre_two, weight, head))
    (slopes,) = call(score_body, [((8, 6, 32, 128), BF)], [], 0, vals, obs, name="score")
    slopes = trade(slopes, MEM)
    slope, head_grad, edges, sent = call(
        slope_body,
        [ACT, ((256, 128), F32), EDGES, POST],
        [((12, 96, 256), BF), ((6, 256, 128), BF), ((192, 256), BF), ACT],
        1,
        *(tab, slopes, head, pre_two, weight),
        name="slope",
        us=4,
    )
    got = trade(sent, ("zl", "y"))
    keep_two, give_two, inner = call(
        back_body,
        [((8, 8, 20, 256), F32), ((8, 8, 20, 256), F32), ACT],
        [((2304, 256), F32), ((3, 6, 288, 256), BF), ((576, 256), BF)],
        1,
        *(core, wide_mid, slope, head_grad, weight),
        name="back",
        us=6,
    )
    got_two = swap(give_two, "c", 2, 1)
    got, inner, got_two = lax.optimization_barrier((got, inner, got_two))
    near = exchange(tab, over, edges, got)
    keep_one, give_one = call(
        first_body,
        [((8, 144, 256), F32), ((8, 144, 256), F32)],
        [((6, 64, 256), BF), ((6, 256, 256), BF), ((2304, 256), F32)],
        2,
        *(tab, core, *near, inner, pre_one, wide_in),
        name="first",
        us=4,
    )
    got_one = swap(give_one, "c", 2, 1)
    (packed,) = call(
        pack_body, [((64, 38, 256), F32)], [], 0, keep_one, got_one, keep_two, got_two, name="pack"
    )
    return call(add_body, [((18, 2, 256), F32), ((2, 80), F32)], [], 0, trade(packed, CORE), name="add")


def solution(mesh):
    fine = Mesh(mesh.devices.reshape(2, 4, 2, 2, 4), FACE + MEM)
    both = FACE + MEM
    in_specs = (P(MEM, FACE), P(FACE, None, MEM), P(both), P(both), P(), P())
    return jax.shard_map(
        shards, mesh=fine, in_specs=in_specs, out_specs=(P(both), P(both)), check_vma=False
    )
```
